128 devices in a mesh: docs: 32 (over z, y, core), split: 4 (over x).
Axes of the slice: x: 4, y: 4, z: 4, core: 2. Of those that a mesh axis runs over, the one named last changes fastest.
Arguments:
- embeddings: float32 [131072, 768], P(('docs', 'split'))
- cluster_id: int32 [131072], P(('docs', 'split')), may hold values from 0 to 127, as said below
Outputs:
- best_similarity: float32 [131072], P(('docs', 'split'))
The draws below stay inside these ranges and needn't reach their ends.
Inputs may be any that keep to these rules, and one draw needn't show every extreme that they name: `cluster_id`: documents are in blocks of 1024 rows, one block a device in order. In every block at most 64 documents have ids in any one range k * 4 to (k + 1) * 4 - 1, and in every draw one such range holds exactly 64 documents of every block.
All inputs are finite; a program needn't handle non-finite values.
Results may differ from the reference program's by a relative error of at most 0.0003.
Values may be sent and summed in bfloat16 or wider, within the bound.
No kernel may reach another device: no remote copies, remote signals or barrier semaphores. Data moves between devices by JAX's collectives and lax.ppermute only.
A program may use at most 128 MiB of HBM per device.

```python
import jax
import jax.numpy as jnp
from jax import lax

E = 768
DOC_DEV = 1024
CLU_DEV = 4
SEND_CAP = 64
TOTAL = 131072
N_DOCS = 32
N_SPLIT = 4
DEVICES = 128


def draw_cluster_id(key, part):
    key = jax.random.fold_in(key, 3)
    hot_owner = jax.random.randint(jax.random.fold_in(key, 1), (), 0, N_DOCS)

    def one_device(device_key):
        key_slots, key_pick, key_order = jax.random.split(device_key, 3)
        others = jax.random.permutation(key_slots, (N_DOCS - 1) * SEND_CAP)[:DOC_DEV - SEND_CAP] // SEND_CAP
        others = (others + (others >= hot_owner).astype(jnp.int32)).astype(jnp.int32)
        target = jnp.concatenate([jnp.full((SEND_CAP,), hot_owner, jnp.int32), others])
        picked = jnp.min(jax.random.randint(key_pick, (3, DOC_DEV), 0, CLU_DEV), axis=0)
        cluster = (target * CLU_DEV + picked).astype(jnp.int32)
        return jax.random.permutation(key_order, cluster)
    device_keys = jax.random.split(jax.random.fold_in(key, 2), DEVICES)
    return jax.vmap(one_device)(device_keys).reshape(-1).astype(jnp.int32)


def draw_embeddings(key, part):
    key = jax.random.fold_in(key, 5)
    key_table, key_which, key_noise, key_scale = jax.random.split(key, 4)
    topics = DOC_DEV * N_SPLIT // CLU_DEV
    table = jax.random.normal(key_table, (topics, E), jnp.float32)
    which = jax.random.randint(key_which, (TOTAL,), 0, topics)
    noise = jax.random.normal(key_noise, (TOTAL, E), jnp.float32)
    scaling = jnp.exp(jax.random.uniform(key_scale, (TOTAL, 1), jnp.float32, 0.0, 2.3025851))
    return (scaling * (noise + 2.0 * table[which])).astype(jnp.float32)


def setup_inputs(seed: int = 0) -> dict:
    splits = jax.random.split(jax.random.key(seed), 3)
    return {
        "embeddings": draw_embeddings(jax.random.fold_in(splits[2], 71), 0),
        "cluster_id": draw_cluster_id(jax.random.fold_in(splits[2], 71), 0),
    }


epsilon = 1e-06

def unit_rows(rows):
    columns = rows.shape[1]
    scaling = lax.rsqrt(lax.optimization_barrier(jnp.mean(rows * rows, axis=1, keepdims=True)) + epsilon) * columns ** (-0.5)
    return (rows * scaling).astype(jnp.bfloat16)

def reference(embeddings, cluster_id):
    normed = unit_rows(embeddings)
    target = cluster_id // CLU_DEV
    ordering = jnp.argsort(target, stable=True).astype(jnp.int32)
    counts = lax.optimization_barrier(jnp.sum((target[:, None] == jnp.arange(N_DOCS, dtype=jnp.int32)[None, :]).astype(jnp.int32), axis=0))
    starts = (jnp.cumsum(counts) - counts).astype(jnp.int32)
    window = DEVICES * SEND_CAP
    padded_rows = jnp.concatenate([normed[ordering].astype(jnp.float32), jnp.zeros((window, E), jnp.float32)], axis=0)
    padded_ids = jnp.concatenate([cluster_id[ordering], jnp.full((window,), -1, jnp.int32)], axis=0)
    block_len = min(window, 1024)
    block_count = window // block_len

    def owner_best(start_at):
        window_rows = lax.dynamic_slice_in_dim(padded_rows, start_at, window, 0)
        window_ids = lax.dynamic_slice_in_dim(padded_ids, start_at, window, 0)
        window_pos = jnp.arange(window, dtype=jnp.int32)

        def row_block(blockargs):
            own_rows, own_ids, own_pos = blockargs
            scores = jnp.dot(own_rows, window_rows.T, precision=lax.Precision.HIGHEST, preferred_element_type=jnp.float32)
            allowed = (own_ids[:, None] == window_ids[None, :]) & (own_pos[:, None] != window_pos[None, :]) & (own_ids[:, None] >= 0)
            return lax.optimization_barrier(jnp.max(jnp.where(allowed, scores, jnp.float32(-1.0)), axis=1))
        blocks = (window_rows.reshape(block_count, block_len, E), window_ids.reshape(block_count, block_len), window_pos.reshape(block_count, block_len))
        return lax.map(row_block, blocks).reshape(window)
    values = lax.map(owner_best, starts)
    offsets = jnp.arange(window, dtype=jnp.int32)[None, :]
    indices = jnp.where(offsets < counts[:, None], starts[:, None] + offsets, TOTAL).astype(jnp.int32)
    sorted_best = jnp.full((TOTAL,), -1.0, jnp.float32).at[indices.reshape(-1)].set(values.reshape(-1), mode='drop')
    return jnp.zeros((TOTAL,), jnp.float32).at[ordering].set(sorted_best)
```

```python
import jax
import jax.numpy as jnp
from jax import lax
from jax.experimental import pallas as pl
from jax.experimental.pallas import tpu as pltpu
from jax.sharding import PartitionSpec as P

F32 = jnp.float32
BF16 = jnp.bfloat16
CLU_DEV = 4
EPSILON = 1e-06
CAP = 64
T = 16
CHUNKS = CAP // T
GROUPS = ((0,), (1,), (2,), (3,))
X1_CHUNKS = (0, 1)
X2_CHUNKS = (2, 3)
AXES = ("docs", "split")
NT = (((1,), (1,)), ((), ()))
NN = (((1,), (0,)), ((), ()))
VMEM = pl.BlockSpec(memory_space=pltpu.VMEM)
SMEM = pl.BlockSpec(memory_space=pltpu.SMEM)
HBM = pl.BlockSpec(memory_space=pl.ANY)
PARAMS = pltpu.CompilerParams(vmem_limit_bytes=48 * 2**20)


def iota(shape, axis):
    return lax.broadcasted_iota(jnp.int32, shape, axis)


def place(unit, rng, rank, owners, chunk):
    inside = (rank >= chunk * T) & (rank < (chunk + 1) * T)
    row = jnp.where(inside, rng * T + rank - chunk * T, -1)
    pick = jnp.where(iota((owners * T, row.shape[1]), 0) == row, 1.0, 0.0).astype(BF16)
    return lax.dot_general(pick, unit, NN, preferred_element_type=F32).astype(BF16)


def prepare(owners, split, ids_ref, emb_ref, pos_ref, unit_ref, first_ref, sent_ids_ref, emb, sems):
    docs, columns = emb.shape
    parts = 4
    size = docs // parts
    copies = [
        pltpu.make_async_copy(emb_ref.at[pl.ds(p * size, size)], emb.at[pl.ds(p * size, size)], sems.at[p])
        for p in range(parts)
    ]
    for copy in copies:
        copy.start()
    ids = ids_ref[...]
    rng = ids >> 2
    key = (ids * docs + iota(ids.shape, 1)).astype(F32)
    base = (rng * (CLU_DEV * docs)).astype(F32)
    key_col = jnp.transpose(jnp.broadcast_to(key, (128, docs)))
    ranks = []
    for lane in range(0, docs, 128):
        before = (key_col < key[:, lane : lane + 128]) & (key_col >= base[:, lane : lane + 128])
        ranks.append(jnp.sum(jnp.where(before, 1.0, 0.0), axis=0, keepdims=True))
    rank = jnp.concatenate(ranks, axis=1).astype(jnp.int32)
    pos_ref[0:1, :] = rng
    pos_ref[1:2, :] = rank
    owner = jnp.where(iota((owners * split, docs), 0) // split == rng, 1.0, 0.0).astype(BF16)
    code = jnp.where(iota((CAP, docs), 0) == rank, (ids & 3) + 1, 0).astype(F32).astype(BF16)
    sent_ids_ref[...] = lax.dot_general(owner, code, NT, preferred_element_type=F32)
    for p in range(parts):
        copies[p].wait()
        rows = emb[p * size : (p + 1) * size, :]
        scaling = lax.rsqrt(jnp.mean(rows * rows, axis=1, keepdims=True) + EPSILON) * columns ** (-0.5)
        unit_ref[p * size : (p + 1) * size, :] = (rows * scaling).astype(BF16)
    first_ref[...] = place(unit_ref[...], rng, rank, owners, 0)


def place_rest(owners, pos_ref, unit_ref, *outs):
    unit = unit_ref[...]
    for chunk, out in enumerate(outs, start=1):
        out[...] = place(unit, pos_ref[0:1, :], pos_ref[1:2, :], owners, chunk)


def slot_ids(split, owners, roles_ref, got_ref, ids_ref):
    got = got_ref[...]
    width = owners * T
    for chunk in range(CHUNKS):
        spread = jnp.where(iota((CAP, width), 0) == chunk * T + iota((CAP, width), 1) % T, 1.0, 0.0).astype(BF16)
        wide = lax.dot_general(got.astype(BF16), spread, NN, preferred_element_type=F32)
        source = iota((owners * split, width), 0) - iota((owners * split, width), 1) // T * split
        for role in range(4):
            codes = jnp.sum(jnp.where(source == roles_ref[role], wide, 0.0), axis=0, keepdims=True)
            block = role * CHUNKS + chunk
            ids_ref[block : block + 1, :] = codes * roles_ref[4 + role].astype(F32)


def scores(names, pairs, fresh, *refs):
    ids_ref, best_in_ref = refs[0], refs[1]
    blocks = dict(zip(names, refs[2 : 2 + len(names)]))
    best_ref = refs[2 + len(names)]
    best_ref[...] = jnp.full(best_ref.shape, -1.0, F32) if fresh else best_in_ref[...]
    width = best_ref.shape[1]

    def into(block, values):
        best_ref[block : block + 1, :] = jnp.maximum(best_ref[block : block + 1, :], values)

    for left in dict.fromkeys(p[0] for p in pairs):
        ids_left = ids_ref[left : left + 1, :]
        ids_rows = jnp.transpose(jnp.broadcast_to(jnp.where(ids_left > 0, ids_left, -1.0), (128, width)))[:, :1]
        total = None
        for right in [p[1] for p in pairs if p[0] == left]:
            score = lax.dot_general(blocks[left][...], blocks[right][...], NT, preferred_element_type=F32)
            allowed = ids_rows == ids_ref[right : right + 1, :]
            if left == right:
                allowed = allowed & (iota((width, width), 0) != iota((width, width), 1))
            score = jnp.where(allowed, score, -1.0)
            into(right, jnp.max(score, axis=0, keepdims=True))
            if left != right:
                for lane in range(0, width, 128):
                    part = score[:, lane : lane + 128]
                    total = part if total is None else jnp.maximum(total, part)
        if total is not None:
            into(left, jnp.max(jnp.transpose(total), axis=0, keepdims=True))


def pack(split, owners, roles_ref, best_ref, out_ref):
    width = best_ref.shape[1]
    rows = owners * split
    source = iota((rows, width), 0) - iota((rows, width), 1) // T * split
    result = jnp.zeros((rows, CAP), F32)
    for chunk in range(CHUNKS):
        wide = jnp.zeros((rows, width), F32)
        for role in range(4):
            block = role * CHUNKS + chunk
            wide = jnp.where(source == roles_ref[role], best_ref[block : block + 1, :], wide)
        narrow = jnp.where(iota((width, CAP), 1) == chunk * T + iota((width, CAP), 0) % T, 1.0, 0.0)
        result = result + lax.dot_general(
            wide, narrow, NN, precision=lax.Precision.HIGHEST, preferred_element_type=F32
        )
    out_ref[...] = result


def finish(owners, split, pos_ref, got_ref, out_ref):
    best = got_ref[pl.ds(0, owners, stride=split), :]
    for part in range(1, split):
        best = jnp.maximum(best, got_ref[pl.ds(part, owners, stride=split), :])
    rng, rank = pos_ref[0:1, :], pos_ref[1:2, :]
    docs = rng.shape[1]
    pick = jnp.where(iota((owners, docs), 0) == rng, 1.0, 0.0)
    columns = lax.dot_general(
        best, pick, (((0,), (0,)), ((), ())), precision=lax.Precision.HIGHEST, preferred_element_type=F32
    )
    out_ref[...] = jnp.sum(jnp.where(iota((CAP, docs), 0) == rank, columns, 0.0), axis=0, keepdims=True)


def ring_moves(owners, split):
    def moves(pairs):
        out = []
        for d in range(owners):
            for a, b in pairs:
                if d % 2:
                    a, b = (2 - a) % split, (2 - b) % split
                out.append((d * split + a % split, d * split + b % split))
        return out

    return moves([(a, a - 1) for a in range(split)]), moves([(1, 0), (2, 1)]), moves([(2, 3), (3, 0)])


def per_device(embeddings, cluster_id):
    docs, columns = embeddings.shape
    owners, split = lax.axis_size("docs"), lax.axis_size("split")
    width = owners * T
    block = jax.ShapeDtypeStruct((width, columns), BF16)
    odd, place_x = lax.axis_index("docs") % 2, lax.axis_index("split")
    step = 1 - 2 * odd
    mirrored = jnp.where(odd == 1, (2 - place_x) % split, place_x)
    roles = jnp.stack(
        [
            place_x,
            (place_x + step) % split,
            (place_x + 2) % split,
            (place_x - step) % split,
            1,
            1,
            (mirrored <= 1).astype(jnp.int32),
            ((mirrored == 3) | (mirrored == 0)).astype(jnp.int32),
        ]
    ).astype(jnp.int32)

    pos, unit, first, sent_ids = pl.pallas_call(
        lambda *refs: prepare(owners, split, *refs),
        in_specs=[VMEM, HBM],
        out_specs=[VMEM] * 4,
        out_shape=[
            jax.ShapeDtypeStruct((2, docs), jnp.int32),
            jax.ShapeDtypeStruct((docs, columns), BF16),
            block,
            jax.ShapeDtypeStruct((owners * split, CAP), F32),
        ],
        scratch_shapes=[pltpu.VMEM((docs, columns), F32), pltpu.SemaphoreType.DMA((4,))],
        compiler_params=PARAMS,
        name="prepare",
    )(cluster_id.reshape(1, docs), embeddings)
    rest = pl.pallas_call(
        lambda *refs: place_rest(owners, *refs),
        in_specs=[VMEM, VMEM],
        out_specs=[VMEM] * (CHUNKS - 1),
        out_shape=[block] * (CHUNKS - 1),
        compiler_params=PARAMS,
        name="place_rest",
    )(pos, unit)
    placed = [first, *rest]

    def to_owner(x):
        return lax.all_to_all(x.reshape(owners, T, columns), "docs", 0, 0, tiled=True).reshape(width, columns)

    own = [to_owner(x) for x in placed]
    got_ids = lax.all_to_all(sent_ids, AXES, 0, 0, tiled=True)
    ids = pl.pallas_call(
        lambda *refs: slot_ids(split, owners, *refs),
        in_specs=[SMEM, VMEM],
        out_specs=VMEM,
        out_shape=jax.ShapeDtypeStruct((4 * CHUNKS, width), F32),
        compiler_params=PARAMS,
        name="slot_ids",
    )(roles, got_ids)

    moves_n, moves_1, moves_2 = ring_moves(owners, split)
    near = [lax.ppermute(x, AXES, moves_n) for x in own]
    held = {c: x for c, x in enumerate(own)}
    held |= {CHUNKS + c: x for c, x in enumerate(near)}
    held |= {2 * CHUNKS + c: lax.ppermute(near[c], AXES, moves_1) for c in X1_CHUNKS}
    held |= {3 * CHUNKS + c: lax.ppermute(own[c], AXES, moves_2) for c in X2_CHUNKS}

    def score_call(best, pairs, name):
        names = sorted({b for p in pairs for b in p})
        return pl.pallas_call(
            lambda *refs: scores(names, pairs, best is None, *refs),
            in_specs=[VMEM] * (2 + len(names)),
            out_specs=VMEM,
            out_shape=jax.ShapeDtypeStruct((4 * CHUNKS, width), F32),
            compiler_params=PARAMS,
            name=name,
        )(ids, ids if best is None else best, *[held[b] for b in names])

    every = range(CHUNKS)
    best = score_call(None, [(a, b) for a in every for b in every if a <= b], "own_own")
    best = score_call(best, [(a, CHUNKS + b) for a in every for b in (0, 1)], "own_near01")
    best = score_call(
        best, [(a, b) for a in every for b in (2 * CHUNKS, 2 * CHUNKS + 1, CHUNKS + 2)], "own_far01_near2"
    )
    best = score_call(
        best,
        [(a, CHUNKS + 3) for a in every] + [(CHUNKS + a, 3 * CHUNKS + b) for a in every for b in X2_CHUNKS],
        "last",
    )
    sent_best = pl.pallas_call(
        lambda *refs: pack(split, owners, *refs),
        in_specs=[SMEM, VMEM],
        out_specs=VMEM,
        out_shape=jax.ShapeDtypeStruct((owners * split, CAP), F32),
        compiler_params=PARAMS,
        name="pack",
    )(roles, best)
    got_best = lax.all_to_all(sent_best, AXES, 0, 0, tiled=True)
    out = pl.pallas_call(
        lambda *refs: finish(owners, split, *refs),
        in_specs=[VMEM, VMEM],
        out_specs=VMEM,
        out_shape=jax.ShapeDtypeStruct((1, docs), F32),
        compiler_params=PARAMS,
        name="finish",
    )(pos, got_best)
    return out.reshape(docs)


def solution(mesh):
    return jax.shard_map(
        per_device,
        mesh=mesh,
        in_specs=(P(AXES, None), P(AXES)),
        out_specs=P(AXES),
        check_vma=False,
    )
```

```python
import jax
import jax.numpy as jnp
from jax import lax
from jax.experimental import pallas as pl
from jax.experimental.pallas import tpu as pltpu
from jax.sharding import PartitionSpec as P

F32 = jnp.float32
BF16 = jnp.bfloat16
CLU_DEV = 4
EPSILON = 1e-06
SIDE = 4
PEERS = SIDE * SIDE
CAP = 64
LANES = 128
CODE_ROWS = 16
CHUNKS = ((0, 0, 64), (1, 0, 32), (1, 32, 32))
STEP = 32
ROWS = 16
OWN, NEAR, FAR = 0, 1, 2
AXES = ("docs", "split")
NT = (((1,), (1,)), ((), ()))
NN = (((1,), (0,)), ((), ()))
VMEM = pl.BlockSpec(memory_space=pltpu.VMEM)
SMEM = pl.BlockSpec(memory_space=pltpu.SMEM)
HBM = pl.BlockSpec(memory_space=pl.ANY)
PARAMS = pltpu.CompilerParams(vmem_limit_bytes=48 * 2**20)


def iota(shape, axis):
    return lax.broadcasted_iota(jnp.int32, shape, axis)


def flat(x, y, z, core):
    return ((z % SIDE * SIDE + y % SIDE) * 2 + core) * SIDE + x % SIDE


def plane_groups():
    side = range(SIDE)
    first = [[flat(x, y, z, 0) for z in side for y in side] for x in side]
    return first + [[flat(x, y, z, 1) for z in side for x in side] for y in side]


def line_moves(steps):
    side = range(SIDE)
    out = [(flat(a, u, z, 0), flat(b, u, z, 0)) for a, b in steps for u in side for z in side]
    return out + [(flat(u, a, z, 1), flat(u, b, z, 1)) for a, b in steps for u in side for z in side]


def core_moves():
    side = range(SIDE)
    return [(flat(x, y, z, c), flat(x, y, z, 1 - c)) for x in side for y in side for z in side for c in (0, 1)]


def chunk_shape(width, columns):
    return (PEERS, width * columns // LANES + CODE_ROWS, LANES)


def place(unit, kind_rng, rank, ids, chunk, out):
    kind, low, width = chunk
    docs, columns = unit.shape
    inside = (kind_rng >= kind * PEERS) & (kind_rng < (kind + 1) * PEERS) & (rank >= low) & (rank < low + width)
    row = jnp.where(inside, (kind_rng - kind * PEERS) * width + rank - low, -1)
    pick = jnp.where(iota((PEERS * width, docs), 0) == row, 1.0, 0.0).astype(BF16)
    rows = lax.dot_general(pick, unit, NN, preferred_element_type=F32).astype(BF16)
    for tile in range(columns // LANES):
        part = rows[:, tile * LANES : (tile + 1) * LANES]
        out[:, tile * width : (tile + 1) * width, :] = part.reshape(PEERS, width, LANES)
    peer = iota((PEERS * CODE_ROWS, docs), 0) // CODE_ROWS
    owner = jnp.where(inside & (kind_rng - kind * PEERS == peer), 1.0, 0.0).astype(BF16)
    code = jnp.where(iota((LANES, docs), 0) == rank - low, (ids & (CLU_DEV - 1)) + 1, 0).astype(F32).astype(BF16)
    codes = lax.dot_general(owner, code, NT, preferred_element_type=F32).astype(BF16)
    out[:, width * columns // LANES :, :] = codes.reshape(PEERS, CODE_ROWS, LANES)


def prepare(here_ref, ids_ref, emb_ref, pos_ref, unit_ref, first_ref, emb, sems):
    docs, columns = emb.shape
    parts = 4
    size = docs // parts
    copies = [
        pltpu.make_async_copy(emb_ref.at[pl.ds(p * size, size)], emb.at[pl.ds(p * size, size)], sems.at[p])
        for p in range(parts)
    ]
    for copy in copies:
        copy.start()
    ids = ids_ref[...]
    rng = ids >> 2
    key = (ids * docs + iota(ids.shape, 1)).astype(F32)
    base = (rng * (CLU_DEV * docs)).astype(F32)
    key_col = jnp.transpose(jnp.broadcast_to(key, (LANES, docs)))
    ranks = []
    for lane in range(0, docs, LANES):
        before = (key_col < key[:, lane : lane + LANES]) & (key_col >= base[:, lane : lane + LANES])
        ranks.append(jnp.sum(jnp.where(before, 1.0, 0.0), axis=0, keepdims=True))
    rank = jnp.concatenate(ranks, axis=1).astype(jnp.int32)
    kind_rng = rng ^ (here_ref[0] * PEERS)
    pos_ref[0:1, :] = rng
    pos_ref[1:2, :] = rank
    pos_ref[2:3, :] = kind_rng
    pos_ref[3:4, :] = ids
    for p in range(parts):
        copies[p].wait()
        rows = emb[p * size : (p + 1) * size, :]
        scaling = lax.rsqrt(jnp.mean(rows * rows, axis=1, keepdims=True) + EPSILON) * columns ** (-0.5)
        unit_ref[p * size : (p + 1) * size, :] = (rows * scaling).astype(BF16)
    place(unit_ref[...], kind_rng, rank, ids, CHUNKS[0], first_ref)


def place_rest(pos_ref, unit_ref, *outs):
    unit = unit_ref[...]
    rank, kind_rng, ids = pos_ref[1:2, :], pos_ref[2:3, :], pos_ref[3:4, :]
    for chunk, out in zip(CHUNKS[1:], outs):
        place(unit, kind_rng, rank, ids, chunk, out)


def lane_slot(width):
    lane = iota((1, PEERS * width), 1)
    return lane // STEP % PEERS, lane // (STEP * PEERS) * STEP + lane % STEP


def chunk_codes(ref, width):
    codes = ref[:, ref.shape[1] - CODE_ROWS :, :].astype(F32)[:, 0, :].astype(BF16)
    peer, slot = lane_slot(width)
    spread = jnp.where(iota((LANES, PEERS * width), 0) == slot, 1.0, 0.0).astype(BF16)
    wide = lax.dot_general(codes, spread, NN, preferred_element_type=F32)
    return jnp.sum(jnp.where(iota(wide.shape, 0) == peer, wide, 0.0), axis=0, keepdims=True)


def block_rows(ref, width, step):
    tiles = (ref.shape[1] - CODE_ROWS) // width
    parts = [ref[:, t * width + step * STEP : t * width + (step + 1) * STEP, :] for t in range(tiles)]
    return jnp.concatenate([p.reshape(PEERS * STEP, LANES) for p in parts], axis=1)


def scores(names, pairs, fresh, here_ref, best_in_ref, *refs):
    chunks = dict(zip(names, refs[: len(names)]))
    best_ref = refs[len(names)]
    best_ref[...] = jnp.full(best_ref.shape, -1.0, F32) if fresh else best_in_ref[...]
    size = PEERS * STEP
    width = {n: CHUNKS[n[1]][2] for n in names}
    codes = {n: chunk_codes(chunks[n], width[n]) for n in names}

    def into(name, step, values):
        row = name[0] * len(CHUNKS) + name[1]
        at = (slice(row, row + 1), slice(step * size, (step + 1) * size))
        best_ref[at] = jnp.maximum(best_ref[at], values)

    def run(some):
        for left in dict.fromkeys(p[0] for p in some):
            for i in range(width[left] // STEP):
                left_rows = block_rows(chunks[left], width[left], i)
                left_codes = codes[left][:, i * size : (i + 1) * size]
                left_codes = jnp.where(left_codes > 0, left_codes, -1.0)
                left_codes = jnp.transpose(jnp.broadcast_to(left_codes, (LANES, size)))[:, :1]
                total = None
                for right in [p[1] for p in some if p[0] == left]:
                    for j in range(width[right] // STEP):
                        if left == right and j < i:
                            continue
                        right_rows = block_rows(chunks[right], width[right], j)
                        score = lax.dot_general(left_rows, right_rows, NT, preferred_element_type=F32)
                        allowed = left_codes == codes[right][:, j * size : (j + 1) * size]
                        same = left == right and i == j
                        if same:
                            allowed = allowed & (iota((size, size), 0) != iota((size, size), 1))
                        score = jnp.where(allowed, score, -1.0)
                        into(right, j, jnp.max(score, axis=0, keepdims=True))
                        if not same:
                            for lane in range(0, size, LANES):
                                part = score[:, lane : lane + LANES]
                                total = part if total is None else jnp.maximum(total, part)
                if total is not None:
                    into(left, i, jnp.max(jnp.transpose(total), axis=0, keepdims=True))

    run([p for p in pairs if p[1][0] != FAR])
    far = [p for p in pairs if p[1][0] == FAR]
    if far:
        pl.when(here_ref[2] > 0)(lambda: run(far))


def pack(here_ref, best_ref, out_ref):
    core, spot = here_ref[0], here_ref[1]
    devices = out_ref.shape[0]
    result = jnp.zeros(out_ref.shape, F32)
    for number, (kind, low, width) in enumerate(CHUNKS):
        size = PEERS * width
        peer, slot = lane_slot(width)
        from_core = core if kind == 0 else 1 - core
        wide = jnp.zeros((devices, size), F32)
        for role, shift in ((OWN, 0), (NEAR, 1), (FAR, 3), (None, 2)):
            line = (spot + shift) % SIDE
            first = peer * (2 * SIDE) + from_core * SIDE + line
            second = peer // SIDE * (2 * PEERS) + line * (2 * SIDE) + from_core * SIDE + peer % SIDE
            source = jnp.where(core == 0, first, second)
            row = 0 if role is None else role * len(CHUNKS) + number
            values = jnp.full((1, size), -1.0, F32) if role is None else best_ref[row : row + 1, :size]
            wide = jnp.where(iota(wide.shape, 0) == source, values, wide)
        narrow = jnp.where(iota((CAP, size), 0) == slot + low, 1.0, 0.0)
        result = result + lax.dot_general(wide, narrow, NT, precision=lax.Precision.HIGHEST, preferred_element_type=F32)
    out_ref[...] = result


def finish(pos_ref, got_ref, out_ref):
    rng, rank = pos_ref[0:1, :], pos_ref[1:2, :]
    got = got_ref[...]
    devices, docs = got.shape[0], rng.shape[1]
    peer = rng % PEERS
    best = jnp.full((CAP, docs), -1.0, F32)
    for line in range(SIDE):
        first = peer * (2 * SIDE) + line
        second = peer // SIDE * (2 * PEERS) + line * (2 * SIDE) + SIDE + peer % SIDE
        source = jnp.where(rng < PEERS, first, second)
        pick = jnp.where(iota((devices, docs), 0) == source, 1.0, 0.0)
        found = lax.dot_general(
            got, pick, (((0,), (0,)), ((), ())), precision=lax.Precision.HIGHEST, preferred_element_type=F32
        )
        best = jnp.maximum(best, found)
    out_ref[...] = jnp.sum(jnp.where(iota((CAP, docs), 0) == rank, best, 0.0), axis=0, keepdims=True)


def after(x, *others):
    return lax.optimization_barrier((x, *others))[0]


def per_device(embeddings, cluster_id):
    docs, columns = embeddings.shape
    devices = lax.axis_size("docs") * lax.axis_size("split")
    at = lax.axis_index("docs")
    core = at % 2
    spot = jnp.where(core == 0, lax.axis_index("split"), at // 2 % SIDE)
    has_far = ((spot == 3) | (spot == 0)).astype(jnp.int32)
    here = jnp.stack([core, spot, has_far]).astype(jnp.int32)
    shapes = [jax.ShapeDtypeStruct(chunk_shape(c[2], columns), BF16) for c in CHUNKS]

    pos, unit, first = pl.pallas_call(
        prepare,
        in_specs=[SMEM, VMEM, HBM],
        out_specs=[VMEM] * 3,
        out_shape=[
            jax.ShapeDtypeStruct((4, docs), jnp.int32),
            jax.ShapeDtypeStruct((docs, columns), BF16),
            shapes[0],
        ],
        scratch_shapes=[pltpu.VMEM((docs, columns), F32), pltpu.SemaphoreType.DMA((4,))],
        compiler_params=PARAMS,
        name="prepare",
    )(here, cluster_id.reshape(1, docs), embeddings)
    rest = pl.pallas_call(
        place_rest,
        in_specs=[VMEM, VMEM],
        out_specs=[VMEM] * (len(CHUNKS) - 1),
        out_shape=shapes[1:],
        compiler_params=PARAMS,
        name="place_rest",
    )(pos, unit)

    groups = plane_groups()
    moves_near = line_moves([(a, a - 1) for a in range(SIDE)])
    moves_far = line_moves([(2, 3), (3, 0)])
    placed = [first] + [lax.ppermute(x, AXES, core_moves()) for x in rest]
    held = {}
    for number, x in enumerate(placed):
        if number:
            x = after(x, held[OWN, number - 1])
        own = lax.all_to_all(x, AXES, 0, 0, axis_index_groups=groups, tiled=True)
        held[OWN, number] = own
        held[NEAR, number] = lax.ppermute(own, AXES, moves_near)
        held[FAR, number] = lax.ppermute(own, AXES, moves_far)

    def score_call(best, pairs, name):
        names = sorted({n for p in pairs for n in p})
        shape = jax.ShapeDtypeStruct((ROWS, PEERS * CAP), F32)
        return pl.pallas_call(
            lambda *refs: scores(names, pairs, best is None, *refs),
            in_specs=[SMEM, VMEM] + [VMEM] * len(names),
            out_specs=VMEM,
            out_shape=shape,
            compiler_params=PARAMS,
            name=name,
        )(here, pos if best is None else best, *[held[n] for n in names])

    best = None
    for number in range(len(CHUNKS)):
        older = range(number)
        pairs = [((OWN, a), (OWN, number)) for a in older] + [((OWN, number), (OWN, number))]
        pairs += [((OWN, number), (NEAR, a)) for a in older]
        best = score_call(best, pairs, f"own_{number}")
        pairs = [((OWN, a), (NEAR, number)) for a in range(number + 1)]
        pairs += [((NEAR, a), (FAR, number)) for a in range(number + 1)]
        pairs += [((NEAR, number), (FAR, a)) for a in older]
        best = score_call(best, pairs, f"near_{number}")
    sent = pl.pallas_call(
        pack,
        in_specs=[SMEM, VMEM],
        out_specs=VMEM,
        out_shape=jax.ShapeDtypeStruct((devices, CAP), F32),
        compiler_params=PARAMS,
        name="pack",
    )(here, best)
    got = lax.all_to_all(sent, AXES, 0, 0, tiled=True)
    out = pl.pallas_call(
        finish,
        in_specs=[VMEM, VMEM],
        out_specs=VMEM,
        out_shape=jax.ShapeDtypeStruct((1, docs), F32),
        compiler_params=PARAMS,
        name="finish",
    )(pos, got)
    return out.reshape(docs)


def solution(mesh):
    return jax.shard_map(
        per_device,
        mesh=mesh,
        in_specs=(P(AXES, None), P(AXES)),
        out_specs=P(AXES),
        check_vma=False,
    )
```

```python
import functools

import jax
import jax.numpy as jnp
from jax import lax
from jax.experimental import pallas as pl
from jax.experimental.pallas import tpu as pltpu
from jax.sharding import PartitionSpec as P

F32 = jnp.float32
BF16 = jnp.bfloat16
CLU_DEV = 4
EPSILON = 1e-06
SIDE = 4
PEERS = SIDE * SIDE
CAP = 64
LANES = 128
CODE_ROWS = 16
HALF = PEERS // 2
BLOCK = HALF * CAP
ROWS = 8
CHUNKS = ((0, 0, 64), (1, 0, 48), (1, 48, 16))
BLOCKS = (((0, 32), (32, 32)), ((0, 32), (32, 16)), ((0, 16),))
OWN, NEAR, FAR = 0, 1, 2
LIGHT, HEAVY, ALWAYS = 0, 1, 2
AXES = ("docs", "split")
NT = (((1,), (1,)), ((), ()))
NN = (((1,), (0,)), ((), ()))
VMEM = pl.BlockSpec(memory_space=pltpu.VMEM)
SMEM = pl.BlockSpec(memory_space=pltpu.SMEM)
HBM = pl.BlockSpec(memory_space=pltpu.HBM)
PARAMS = pltpu.CompilerParams(vmem_limit_bytes=32 * 2**20)
SCORE_PARAMS = pltpu.CompilerParams(vmem_limit_bytes=28 * 2**20)


def iota(shape, axis):
    return lax.broadcasted_iota(jnp.int32, shape, axis)


def flat(x, y, z, core):
    return ((z % SIDE * SIDE + y % SIDE) * 2 + core) * SIDE + x % SIDE


def plane_groups():
    side = range(SIDE)
    first = [[flat(x, y, z, 0) for z in side for y in side] for x in side]
    return first + [[flat(x, y, z, 1) for z in side for x in side] for y in side]


def line_moves(steps):
    side = range(SIDE)
    out = [(flat(a, u, z, 0), flat(b, u, z, 0)) for a, b in steps for u in side for z in side]
    return out + [(flat(u, a, z, 1), flat(u, b, z, 1)) for a, b in steps for u in side for z in side]


def core_moves():
    side = range(SIDE)
    return [(flat(x, y, z, c), flat(x, y, z, 1 - c)) for x in side for y in side for z in side for c in (0, 1)]


def place(unit, kind_rng, rank, ids, kind, out):
    docs, columns = unit.shape
    owner = kind_rng - kind * PEERS
    inside = (owner >= 0) & (owner < PEERS) & (rank < CAP)
    row = jnp.where(inside, owner * CAP + rank, -1)
    pick = jnp.where(iota((PEERS * CAP, docs), 0) == row, 1.0, 0.0).astype(BF16)
    rows = lax.dot_general(pick, unit, NN, preferred_element_type=F32).astype(BF16)
    for tile in range(columns // LANES):
        part = rows[:, tile * LANES : (tile + 1) * LANES]
        out[:, tile * CAP : (tile + 1) * CAP, :] = part.reshape(PEERS, CAP, LANES)
    code_peer = iota((PEERS * CODE_ROWS, docs), 0) // CODE_ROWS
    owned = jnp.where(owner == code_peer, 1.0, 0.0).astype(BF16)
    code = jnp.where(iota((LANES, docs), 0) == rank, (ids & (CLU_DEV - 1)) + 1, 0).astype(F32).astype(BF16)
    codes = lax.dot_general(owned, code, NT, preferred_element_type=F32).astype(BF16)
    out[:, CAP * columns // LANES :, :] = codes.reshape(PEERS, CODE_ROWS, LANES)


def prepare(here_ref, ids_ref, emb_ref, pos_ref, first_ref, other_ref, emb, unit, sems):
    docs, columns = emb.shape
    parts = 4
    size = docs // parts
    copies = [
        pltpu.make_async_copy(emb_ref.at[pl.ds(p * size, size)], emb.at[pl.ds(p * size, size)], sems.at[p])
        for p in range(parts)
    ]
    for copy in copies:
        copy.start()
    ids = ids_ref[...]
    rng = ids >> 2
    key = (ids * docs + iota(ids.shape, 1)).astype(F32)
    base = (rng * (CLU_DEV * docs)).astype(F32)
    key_col = jnp.transpose(jnp.broadcast_to(key, (LANES, docs)))
    ranks = []
    for lane in range(0, docs, LANES):
        before = (key_col < key[:, lane : lane + LANES]) & (key_col >= base[:, lane : lane + LANES])
        ranks.append(jnp.sum(jnp.where(before, 1.0, 0.0), axis=0, keepdims=True))
    rank = jnp.concatenate(ranks, axis=1).astype(jnp.int32)
    pos_ref[0:1, :] = rng
    pos_ref[1:2, :] = rank
    for p in range(parts):
        copies[p].wait()
        rows = emb[p * size : (p + 1) * size, :]
        scaling = lax.rsqrt(jnp.mean(rows * rows, axis=1, keepdims=True) + EPSILON) * columns ** (-0.5)
        unit[p * size : (p + 1) * size, :] = (rows * scaling).astype(BF16)
    kind_rng = rng ^ (here_ref[0] * PEERS)
    for kind, out in enumerate((first_ref, other_ref)):
        place(unit[...], kind_rng, rank, ids, kind, out)


def slot_codes(ref):
    codes = ref[:, ref.shape[1] - CODE_ROWS :, :].astype(F32)[:, 0, :].astype(BF16)
    lane = iota((1, ref.shape[0] * CAP), 1)
    spread = jnp.where(iota((LANES, lane.shape[1]), 0) == lane % CAP, 1.0, 0.0).astype(BF16)
    wide = lax.dot_general(codes, spread, NN, preferred_element_type=F32)
    return jnp.sum(jnp.where(iota(wide.shape, 0) == lane // CAP, wide, 0.0), axis=0, keepdims=True)


def block_rows(ref, half):
    tiles = (ref.shape[1] - CODE_ROWS) // CAP
    peers = slice(half * HALF, (half + 1) * HALF)
    parts = [ref[peers, t * CAP : (t + 1) * CAP, :].reshape(BLOCK, LANES) for t in range(tiles)]
    return jnp.concatenate(parts, axis=1)


def scores(names, new, pairs, fresh, here_ref, best_in_ref, codes_in_ref, *refs):
    arrays = dict(zip(names, refs[: len(names)]))
    best_ref, codes_ref = refs[len(names) : len(names) + 2]
    if fresh:
        best_ref[...] = jnp.full(best_ref.shape, -1.0, F32)
        codes_ref[...] = jnp.zeros(codes_ref.shape, F32)
    else:
        best_ref[...] = best_in_ref[...]
        codes_ref[...] = codes_in_ref[...]

    def at(block):
        row = block[0] * 2 + block[1]
        return slice(row, row + 1), slice(block[2] * BLOCK, (block[2] + 1) * BLOCK)

    def rows_of(block):
        if block in arrays:
            return block_rows(arrays[block], 0)
        return block_rows(arrays[block[0], block[1], 0], block[2])

    for name in new:
        codes = slot_codes(arrays[name])
        start = name[2] * BLOCK
        codes_ref[at(name)[0], start : start + codes.shape[1]] = codes

    def into(block, values):
        best_ref[at(block)] = jnp.maximum(best_ref[at(block)], values)

    def run(some):
        for left in dict.fromkeys(p[0] for p in some):
            left_rows = rows_of(left)
            left_codes = codes_ref[at(left)]
            left_codes = jnp.where(left_codes > 0, left_codes, -1.0)
            left_codes = jnp.transpose(jnp.broadcast_to(left_codes, (LANES, BLOCK)))[:, :1]
            total = None
            for right in [p[1] for p in some if p[0] == left]:
                score = lax.dot_general(left_rows, rows_of(right), NT, preferred_element_type=F32)
                allowed = left_codes == codes_ref[at(right)]
                if left == right:
                    allowed = allowed & (iota(score.shape, 0) != iota(score.shape, 1))
                score = jnp.where(allowed, score, -1.0)
                into(right, jnp.max(score, axis=0, keepdims=True))
                if left != right:
                    for lane in range(0, BLOCK, LANES):
                        part = score[:, lane : lane + LANES]
                        total = part if total is None else jnp.maximum(total, part)
            if total is not None:
                into(left, jnp.max(jnp.transpose(total), axis=0, keepdims=True))

    run([p[:2] for p in pairs if p[2] == ALWAYS])
    for when in (HEAVY, LIGHT):
        some = [p[:2] for p in pairs if p[2] == when]
        if some:
            pl.when(here_ref[2] == when)(functools.partial(run, some))
    if len(refs) > len(names) + 2:
        pack(here_ref, best_ref, refs[-1])


def pack(here_ref, best_ref, out_ref):
    core, spot = here_ref[0], here_ref[1]
    out_ref[...] = jnp.full(out_ref.shape, -1.0, F32)
    for kind in range(2):
        from_core = core if kind == 0 else 1 - core
        for role, shift in ((OWN, 0), (NEAR, 1), (FAR, 3)):
            line = (spot + shift) % SIDE
            row = role * 2 + kind
            for peer in range(PEERS):
                first = peer * (2 * SIDE) + from_core * SIDE + line
                second = peer // SIDE * (2 * PEERS) + line * (2 * SIDE) + from_core * SIDE + peer % SIDE
                device = jnp.where(core == 0, first, second)
                out_ref[pl.ds(device, 1), :] = best_ref[row : row + 1, peer * CAP : (peer + 1) * CAP]


def finish(pos_ref, got_ref, out_ref):
    rng, rank = pos_ref[0:1, :], pos_ref[1:2, :]
    docs = rng.shape[1]
    first = got_ref[pl.ds(0, PEERS, stride=2 * SIDE), :]
    for line in range(1, SIDE):
        first = jnp.maximum(first, got_ref[pl.ds(line, PEERS, stride=2 * SIDE), :])
    second = []
    for z in range(SIDE):
        rows = [got_ref[pl.ds(z * 2 * PEERS + line * 2 * SIDE + SIDE, SIDE), :] for line in range(SIDE)]
        second.append(functools.reduce(jnp.maximum, rows))
    best = jnp.concatenate([first] + second, axis=0)
    pick = jnp.where(iota((best.shape[0], docs), 0) == rng, 1.0, 0.0)
    found = lax.dot_general(
        best, pick, (((0,), (0,)), ((), ())), precision=lax.Precision.HIGHEST, preferred_element_type=F32
    )
    out_ref[...] = jnp.sum(jnp.where(iota((CAP, docs), 0) == rank, found, 0.0), axis=0, keepdims=True)


def after(x, *others):
    return lax.optimization_barrier((x, *others))[0]


def per_device(embeddings, cluster_id):
    docs, columns = embeddings.shape
    devices = lax.axis_size("docs") * lax.axis_size("split")
    at = lax.axis_index("docs")
    core = at % 2
    spot = jnp.where(core == 0, lax.axis_index("split"), at // 2 % SIDE)
    heavy = ((spot == 3) | (spot == 0)).astype(jnp.int32)
    here = jnp.stack([core, spot, heavy]).astype(jnp.int32)
    slots = jax.ShapeDtypeStruct((PEERS, CAP * columns // LANES + CODE_ROWS, LANES), BF16)

    pos, first, other = pl.pallas_call(
        prepare,
        in_specs=[SMEM, VMEM, HBM],
        out_specs=[VMEM] * 3,
        out_shape=[jax.ShapeDtypeStruct((2, docs), jnp.int32), slots, slots],
        scratch_shapes=[
            pltpu.VMEM((docs, columns), F32),
            pltpu.VMEM((docs, columns), BF16),
            pltpu.SemaphoreType.DMA((4,)),
        ],
        compiler_params=pltpu.CompilerParams(vmem_limit_bytes=56 * 2**20),
        name="prepare",
    )(here, cluster_id.reshape(1, docs), embeddings)

    groups = plane_groups()
    moves_near = line_moves([(a, a - 1) for a in range(SIDE)])
    moves_far = line_moves([(a, a + 1) for a in range(SIDE)])

    def to_owner(x):
        return lax.all_to_all(x, AXES, 0, 0, axis_index_groups=groups, tiled=True)

    held = {}

    def score_call(state, new, pairs, name, extra=()):
        names = sorted({n if n in held else (n[0], n[1], 0) for p in pairs for n in p[:2]})
        table = jax.ShapeDtypeStruct((ROWS, PEERS * CAP), F32)
        return pl.pallas_call(
            lambda *refs: scores(names, new, pairs, state[0] is pos, *refs),
            in_specs=[SMEM, VMEM, VMEM] + [VMEM] * len(names),
            out_specs=[VMEM] * (2 + len(extra)),
            out_shape=[table, table, *extra],
            compiler_params=SCORE_PARAMS,
            name=name,
        )(here, *state[:2], *[held[n] for n in names])

    def blocks(role, kind):
        return [(role, kind, half) for half in range(2)]

    def every(lefts, rights, when=ALWAYS):
        return [(a, b, when) for a in lefts for b in rights if a[:2] != b[:2] or a <= b]

    own_0, own_1, near_0, far_0 = blocks(OWN, 0), blocks(OWN, 1), blocks(NEAR, 0), blocks(FAR, 0)
    (near_a, near_b), (far_a, far_b) = blocks(NEAR, 1), blocks(FAR, 1)
    own = to_owner(first)
    held[own_0[0]] = own
    held[near_0[0]] = lax.ppermute(own, AXES, moves_near)
    held[far_0[0]] = lax.ppermute(own, AXES, moves_far)
    state = score_call(
        (pos, pos),
        (own_0[0], near_0[0], far_0[0]),
        every(own_0, own_0 + near_0) + every(near_0, far_0, LIGHT),
        "scores_first",
    )
    own = to_owner(lax.ppermute(other, AXES, core_moves()))
    held[own_1[0]] = own

    for near, far, peers in ((near_a, far_a, slice(0, HALF)), (near_b, far_b, slice(HALF, PEERS))):
        held[near] = lax.ppermute(own[peers], AXES, moves_near)
        held[far] = lax.ppermute(own[peers], AXES, moves_far)
    state = score_call(
        state,
        (own_1[0],),
        every(own_0, own_1) + every(own_1, own_1 + near_0),
        "scores_own",
    )
    state = score_call(
        state,
        (near_a, far_a),
        every(own_0 + own_1, [near_a]) + every([near_a], far_0) + every([near_a], [far_a], HEAVY),
        "scores_near_a",
    )
    state = score_call(
        state,
        (near_b, far_b),
        every(own_0 + own_1, [near_b])
        + every([near_b], far_0)
        + every([near_b], [far_a, far_b], HEAVY)
        + every([near_a], [far_b], HEAVY),
        "scores_near_b",
        (jax.ShapeDtypeStruct((devices, CAP), F32),),
    )
    got = lax.all_to_all(state[2], AXES, 0, 0, tiled=True)
    out = pl.pallas_call(
        finish,
        in_specs=[VMEM, VMEM],
        out_specs=VMEM,
        out_shape=jax.ShapeDtypeStruct((1, docs), F32),
        compiler_params=PARAMS,
        name="finish",
    )(pos, got)
    return out.reshape(docs)


def solution(mesh):
    return jax.shard_map(
        per_device,
        mesh=mesh,
        in_specs=(P(AXES, None), P(AXES)),
        out_specs=P(AXES),
        check_vma=False,
    )
```

```python
import functools

import jax
import jax.numpy as jnp
from jax import lax
from jax.experimental import pallas as pl
from jax.experimental.pallas import tpu as pltpu
from jax.sharding import PartitionSpec as P

F32 = jnp.float32
BF16 = jnp.bfloat16
CLU_DEV = 4
EPSILON = 1e-06
SIDE = 4
PEERS = SIDE * SIDE
CAP = 64
LANES = 128
CODE_ROWS = 16
HALF = PEERS // 2
ROWS = 8
CHUNKS = ((0, 0, 64), (1, 0, 48), (1, 48, 16))
BLOCKS = (((0, 32), (32, 32)), ((0, 32), (32, 16)), ((0, 16),))
OWN, NEAR, FAR = 0, 1, 2
LIGHT, HEAVY, ALWAYS = 0, 1, 2
AXES = ("docs", "split")
NT = (((1,), (1,)), ((), ()))
NN = (((1,), (0,)), ((), ()))
VMEM = pl.BlockSpec(memory_space=pltpu.VMEM)
HBM = pl.BlockSpec(memory_space=pltpu.HBM)
PARAMS = pltpu.CompilerParams(vmem_limit_bytes=24 * 2**20)
SCORE_PARAMS = pltpu.CompilerParams(vmem_limit_bytes=28 * 2**20)


def iota(shape, axis):
    return lax.broadcasted_iota(jnp.int32, shape, axis)


def flat(x, y, z, core):
    return ((z % SIDE * SIDE + y % SIDE) * 2 + core) * SIDE + x % SIDE


def plane_groups():
    side = range(SIDE)
    first = [[flat(x, y, z, 0) for z in side for y in side] for x in side]
    return first + [[flat(x, y, z, 1) for z in side for x in side] for y in side]


def line_moves(steps):
    side = range(SIDE)
    out = [(flat(a, u, z, 0), flat(b, u, z, 0)) for a, b in steps for u in side for z in side]
    return out + [(flat(u, a, z, 1), flat(u, b, z, 1)) for a, b in steps for u in side for z in side]


def core_moves():
    side = range(SIDE)
    return [(flat(x, y, z, c), flat(x, y, z, 1 - c)) for x in side for y in side for z in side for c in (0, 1)]


def own_core():
    return lax.axis_index("docs") & 1


def own_spot():
    return jnp.where(own_core() == 0, lax.axis_index("split"), (lax.axis_index("docs") >> 1) & (SIDE - 1))


def place(unit, kind_rng, rank, ids, kind, out):
    docs, columns = unit.shape
    owner = kind_rng - kind * PEERS
    inside = (owner >= 0) & (owner < PEERS) & (rank < CAP)
    row = jnp.where(inside, owner * CAP + rank, -1)
    pick = jnp.where(iota((PEERS * CAP, docs), 0) == row, 1.0, 0.0).astype(BF16)
    rows = lax.dot_general(pick, unit, NN, preferred_element_type=F32).astype(BF16)
    for tile in range(columns // LANES):
        part = rows[:, tile * LANES : (tile + 1) * LANES]
        out[:, tile * CAP : (tile + 1) * CAP, :] = part.reshape(PEERS, CAP, LANES)
    code_peer = iota((PEERS * CODE_ROWS, docs), 0) // CODE_ROWS
    owned = jnp.where(owner == code_peer, 1.0, 0.0).astype(BF16)
    code = jnp.where(iota((LANES, docs), 0) == rank, (ids & (CLU_DEV - 1)) + 1, 0).astype(F32).astype(BF16)
    codes = lax.dot_general(owned, code, NT, preferred_element_type=F32).astype(BF16)
    out[:, CAP * columns // LANES :, :] = codes.reshape(PEERS, CODE_ROWS, LANES)


def prepare(ids_ref, emb_ref, pos_ref, first_ref, other_ref, emb, unit, sems):
    docs, columns = emb.shape
    parts = 4
    size = docs // parts
    copies = [
        pltpu.make_async_copy(emb_ref.at[pl.ds(p * size, size)], emb.at[pl.ds(p * size, size)], sems.at[p])
        for p in range(parts)
    ]
    for copy in copies:
        copy.start()
    ids = ids_ref[...]
    rng = ids >> 2
    key = (ids * docs + iota(ids.shape, 1)).astype(F32)
    base = (rng * (CLU_DEV * docs)).astype(F32)
    key_col = jnp.transpose(jnp.broadcast_to(key, (LANES, docs)))
    ranks = []
    for lane in range(0, docs, LANES):
        before = (key_col < key[:, lane : lane + LANES]) & (key_col >= base[:, lane : lane + LANES])
        ranks.append(jnp.sum(jnp.where(before, 1.0, 0.0), axis=0, keepdims=True))
    rank = jnp.concatenate(ranks, axis=1).astype(jnp.int32)
    pos_ref[0:1, :] = rng
    pos_ref[1:2, :] = rank
    for p in range(parts):
        copies[p].wait()
        rows = emb[p * size : (p + 1) * size, :]
        scaling = lax.rsqrt(jnp.mean(rows * rows, axis=1, keepdims=True) + EPSILON) * columns ** (-0.5)
        unit[p * size : (p + 1) * size, :] = (rows * scaling).astype(BF16)
    kind_rng = rng ^ (own_core() * PEERS)
    for kind, out in enumerate((first_ref, other_ref)):
        place(unit[...], kind_rng, rank, ids, kind, out)


def slot_codes(ref):
    codes = ref[:, ref.shape[1] - CODE_ROWS :, :].astype(F32)[:, 0, :].astype(BF16)
    lane = iota((1, ref.shape[0] * CAP), 1)
    spread = jnp.where(iota((LANES, lane.shape[1]), 0) == lane % CAP, 1.0, 0.0).astype(BF16)
    wide = lax.dot_general(codes, spread, NN, preferred_element_type=F32)
    return jnp.sum(jnp.where(iota(wide.shape, 0) == lane // CAP, wide, 0.0), axis=0, keepdims=True)


def block_rows(ref, start, peers):
    tiles = (ref.shape[1] - CODE_ROWS) // CAP
    parts = [ref[start : start + peers, t * CAP : (t + 1) * CAP, :].reshape(peers * CAP, LANES) for t in range(tiles)]
    return jnp.concatenate(parts, axis=1)


def holder(names, block):
    return next(n for n in names if n[:2] == block[:2] and n[2] <= block[2] < n[2] + n[3])


def scores(names, new, loaded, pairs, fresh, last, best_in_ref, codes_in_ref, *refs):
    arrays = dict(zip(names, refs[: len(names)]))
    refs = list(refs[len(names) :])
    best_ref, codes_ref = refs[:2]
    copies = {}
    for number, name in enumerate(loaded):
        target = refs[2] if name == loaded[-1] else refs[3 + number]
        copies[name] = pltpu.make_async_copy(arrays[name], target, refs[-1].at[number])
        copies[name].start()
        arrays[name] = target
    if fresh:
        best_ref[...] = jnp.full(best_ref.shape, -1.0, F32)
        codes_ref[...] = jnp.zeros(codes_ref.shape, F32)
    else:
        best_ref[...] = best_in_ref[...]
        codes_ref[...] = codes_in_ref[...]

    def at(block):
        role, kind, start, peers = block
        return slice(role * 2 + kind, role * 2 + kind + 1), slice(start * CAP, (start + peers) * CAP)

    def rows_of(block):
        name = holder(names, block)
        return block_rows(arrays[name], block[2] - name[2], block[3])

    def arrive(name):
        if name in copies:
            copies.pop(name).wait()
        codes_ref[at(name)] = slot_codes(arrays[name])

    def into(block, values):
        best_ref[at(block)] = jnp.maximum(best_ref[at(block)], values)

    def run(some):
        for left in dict.fromkeys(p[0] for p in some):
            left_rows = rows_of(left)
            left_codes = codes_ref[at(left)]
            left_codes = jnp.where(left_codes > 0, left_codes, -1.0)
            left_codes = jnp.transpose(jnp.broadcast_to(left_codes, (LANES, left_codes.shape[1])))[:, :1]
            total = None
            for right in [p[1] for p in some if p[0] == left]:
                score = lax.dot_general(left_rows, rows_of(right), NT, preferred_element_type=F32)
                allowed = left_codes == codes_ref[at(right)]
                if left == right:
                    allowed = allowed & (iota(score.shape, 0) != iota(score.shape, 1))
                score = jnp.where(allowed, score, -1.0)
                into(right, jnp.max(score, axis=0, keepdims=True))
                if left != right:
                    for lane in range(0, score.shape[1], LANES):
                        part = score[:, lane : lane + LANES]
                        total = part if total is None else jnp.maximum(total, part)
            if total is not None:
                into(left, jnp.max(jnp.transpose(total), axis=0, keepdims=True))

    waiting = list(new)
    for some in pairs:
        for name in [n for n in waiting if any(holder(names, block) == n for p in some for block in p[:2])]:
            waiting.remove(name)
            arrive(name)
        run([p[:2] for p in some if p[2] == ALWAYS])
        for when in (HEAVY, LIGHT):
            part = [p[:2] for p in some if p[2] == when]
            if part:
                pl.when(((own_spot() + 1) & 2) == 2 * (1 - when))(functools.partial(run, part))
    if last:
        pack(best_ref, refs[2])


def pack(best_ref, out_ref):
    core, spot = own_core(), own_spot()
    out_ref[...] = jnp.full(out_ref.shape, -1.0, F32)
    for kind in range(2):
        from_core = core if kind == 0 else 1 - core
        for role, shift in ((OWN, 0), (NEAR, 1), (FAR, 3)):
            line = (spot + shift) % SIDE
            row = role * 2 + kind
            for peer in range(PEERS):
                first = peer * (2 * SIDE) + from_core * SIDE + line
                second = peer // SIDE * (2 * PEERS) + line * (2 * SIDE) + from_core * SIDE + peer % SIDE
                device = jnp.where(core == 0, first, second)
                out_ref[pl.ds(device, 1), :] = best_ref[row : row + 1, peer * CAP : (peer + 1) * CAP]


def finish(pos_ref, got_ref, out_ref):
    rng, rank = pos_ref[0:1, :], pos_ref[1:2, :]
    docs = rng.shape[1]
    first = got_ref[pl.ds(0, PEERS, stride=2 * SIDE), :]
    for line in range(1, SIDE):
        first = jnp.maximum(first, got_ref[pl.ds(line, PEERS, stride=2 * SIDE), :])
    second = []
    for z in range(SIDE):
        rows = [got_ref[pl.ds(z * 2 * PEERS + line * 2 * SIDE + SIDE, SIDE), :] for line in range(SIDE)]
        second.append(functools.reduce(jnp.maximum, rows))
    best = jnp.concatenate([first] + second, axis=0)
    pick = jnp.where(iota((best.shape[0], docs), 0) == rng, 1.0, 0.0)
    found = lax.dot_general(
        best, pick, (((0,), (0,)), ((), ())), precision=lax.Precision.HIGHEST, preferred_element_type=F32
    )
    out_ref[...] = jnp.sum(jnp.where(iota((CAP, docs), 0) == rank, found, 0.0), axis=0, keepdims=True)


def after(x, *others):
    return lax.optimization_barrier((x, *others))[0]


def per_device(embeddings, cluster_id):
    docs, columns = embeddings.shape
    devices = lax.axis_size("docs") * lax.axis_size("split")
    slots = jax.ShapeDtypeStruct((PEERS, CAP * columns // LANES + CODE_ROWS, LANES), BF16)

    pos, first, other = pl.pallas_call(
        prepare,
        in_specs=[VMEM, HBM],
        out_specs=[VMEM] * 3,
        out_shape=[jax.ShapeDtypeStruct((2, docs), jnp.int32), slots, slots],
        scratch_shapes=[
            pltpu.VMEM((docs, columns), F32),
            pltpu.VMEM((docs, columns), BF16),
            pltpu.SemaphoreType.DMA((4,)),
        ],
        compiler_params=PARAMS,
        name="prepare",
    )(cluster_id.reshape(1, docs), pltpu.with_memory_space_constraint(embeddings, pltpu.HBM))

    groups = plane_groups()
    moves_near = line_moves([(a, a - 1) for a in range(SIDE)])
    moves_far = line_moves([(a, a + 1) for a in range(SIDE)])

    def to_owner(x):
        return lax.all_to_all(x, AXES, 0, 0, axis_index_groups=groups, tiled=True)

    held = {}

    def score_call(state, new, pairs, name, loaded=(), last=False):
        names = sorted({holder(held, n) for some in pairs for p in some for n in p[:2]})
        table = jax.ShapeDtypeStruct((ROWS, PEERS * CAP), F32)
        extra = [jax.ShapeDtypeStruct(held[n].shape, BF16) for n in loaded[-1:]]
        if last:
            extra.append(jax.ShapeDtypeStruct((devices, CAP), F32))
        scratch = [pltpu.VMEM(held[n].shape, BF16) for n in loaded[:-1]]
        if loaded:
            scratch.append(pltpu.SemaphoreType.DMA((len(loaded),)))
        out = pl.pallas_call(
            lambda *refs: scores(names, new, loaded, pairs, state[0] is pos, last, *refs),
            in_specs=[VMEM, VMEM] + [HBM if n in loaded else VMEM for n in names],
            out_specs=[VMEM] * (2 + len(extra)),
            out_shape=[table, table, *extra],
            scratch_shapes=scratch,
            compiler_params=SCORE_PARAMS,
            name=name,
        )(*state[:2], *[held[n] for n in names])
        held.update(zip(loaded[-1:], out[2:]))
        return out

    def blocks(role, kind, start=0, end=PEERS):
        return [(role, kind, p, min(HALF, end - p)) for p in range(start, end, HALF)]

    def every(lefts, rights, when=ALWAYS):
        return [(a, b, when) for a in lefts for b in rights if a[:2] != b[:2] or a <= b]

    own_0, own_1, near_0, far_0 = blocks(OWN, 0), blocks(OWN, 1), blocks(NEAR, 0), blocks(FAR, 0)
    whole_0 = [(role, 0, 0, PEERS) for role in (OWN, NEAR, FAR)]
    own = to_owner(first)
    held[whole_0[0]] = own
    held[whole_0[1]] = lax.ppermute(own, AXES, moves_near)
    held[whole_0[2]] = lax.ppermute(own, AXES, moves_far)
    state = score_call((pos, pos), whole_0[:1], [every(own_0, own_0)], "scores_own_first")
    own = to_owner(lax.ppermute(other, AXES, core_moves()))
    whole_1 = (OWN, 1, 0, PEERS)
    held[whole_1] = own
    own = after(own, state[0])
    parts = ((0, 8), (8, 12), (12, 16))
    for start, end in parts:
        held[NEAR, 1, start, end - start] = lax.ppermute(own[start:end], AXES, moves_near)
        if not start:
            held[FAR, 1, 0, PEERS] = lax.ppermute(own, AXES, moves_far)
    state = score_call(state, (whole_1,), [every(own_0, own_1) + every(own_1, own_1)], "scores_own")
    state = score_call(
        state,
        whole_0[1:],
        [every(own_0 + own_1, near_0), every(near_0[:1], far_0, HEAVY) + every(near_0, far_0[1:], LIGHT)],
        "scores_near_first",
        whole_0[1:],
    )
    for start, end in parts:
        near = blocks(NEAR, 1, start, end)
        new = ((NEAR, 1, start, end - start),)
        pairs = [every(own_0 + own_1, near) + every(near, far_0)]
        if end == PEERS:
            new += ((FAR, 1, 0, PEERS),)
            older = [block for part in parts for block in blocks(NEAR, 1, *part)]
            far_1 = blocks(FAR, 1)
            first_half = [block for block in older if block[2] < HALF]
            pairs.append(every(first_half, far_1, HEAVY) + every(older, far_1[1:], LIGHT))
        state = score_call(state, new, pairs, f"scores_near_{start}", (), end == PEERS)
    got = lax.all_to_all(state[2], AXES, 0, 0, tiled=True)
    out = pl.pallas_call(
        finish,
        in_specs=[VMEM, VMEM],
        out_specs=VMEM,
        out_shape=jax.ShapeDtypeStruct((1, docs), F32),
        compiler_params=PARAMS,
        name="finish",
    )(pos, got)
    return out.reshape(docs)


def solution(mesh):
    return jax.shard_map(
        per_device,
        mesh=mesh,
        in_specs=(P(AXES, None), P(AXES)),
        out_specs=P(AXES),
        check_vma=False,
    )
```

```python
import functools

import jax
import jax.numpy as jnp
from jax import lax
from jax.experimental import pallas as pl
from jax.experimental.pallas import tpu as pltpu
from jax.sharding import PartitionSpec as P

F32 = jnp.float32
BF16 = jnp.bfloat16
CLU_DEV = 4
EPSILON = 1e-06
SIDE = 4
PEERS = SIDE * SIDE
CAP = 64
LANES = 128
CODE_ROWS = 16
HALF = PEERS // 2
ROWS = 8
CHUNKS = ((0, 0, 64), (1, 0, 48), (1, 48, 16))
BLOCKS = (((0, 32), (32, 32)), ((0, 32), (32, 16)), ((0, 16),))
OWN, NEAR, FAR = 0, 1, 2
LIGHT, HEAVY, ALWAYS = 0, 1, 2
AXES = ("docs", "split")
NT = (((1,), (1,)), ((), ()))
NN = (((1,), (0,)), ((), ()))
VMEM = pl.BlockSpec(memory_space=pltpu.VMEM)
HBM = pl.BlockSpec(memory_space=pltpu.HBM)
PARAMS = pltpu.CompilerParams(vmem_limit_bytes=24 * 2**20)
SCORE_PARAMS = pltpu.CompilerParams(vmem_limit_bytes=28 * 2**20)


def iota(shape, axis):
    return lax.broadcasted_iota(jnp.int32, shape, axis)


def flat(x, y, z, core):
    return ((z % SIDE * SIDE + y % SIDE) * 2 + core) * SIDE + x % SIDE


def plane_groups():
    side = range(SIDE)
    first = [[flat(x, y, z, 0) for z in side for y in side] for x in side]
    return first + [[flat(x, y, z, 1) for z in side for x in side] for y in side]


def line_moves(steps):
    side = range(SIDE)
    out = [(flat(a, u, z, 0), flat(b, u, z, 0)) for a, b in steps for u in side for z in side]
    return out + [(flat(u, a, z, 1), flat(u, b, z, 1)) for a, b in steps for u in side for z in side]


def core_moves():
    side = range(SIDE)
    return [(flat(x, y, z, c), flat(x, y, z, 1 - c)) for x in side for y in side for z in side for c in (0, 1)]


def own_core():
    return lax.axis_index("docs") & 1


def own_spot():
    return jnp.where(own_core() == 0, lax.axis_index("split"), (lax.axis_index("docs") >> 1) & (SIDE - 1))


def place(unit, kind_rng, rank, ids, kind, out, peers):
    docs, columns = unit.shape
    count = peers.stop - peers.start
    owner = kind_rng - (kind * PEERS + peers.start)
    inside = (owner >= 0) & (owner < count) & (rank < CAP)
    row = jnp.where(inside, owner * CAP + rank, -1)
    pick = jnp.where(iota((count * CAP, docs), 0) == row, 1.0, 0.0).astype(BF16)
    rows = lax.dot_general(pick, unit, NN, preferred_element_type=F32).astype(BF16)
    for tile in range(columns // LANES):
        part = rows[:, tile * LANES : (tile + 1) * LANES]
        out[peers, tile * CAP : (tile + 1) * CAP, :] = part.reshape(count, CAP, LANES)
    code_peer = iota((count * CODE_ROWS, docs), 0) // CODE_ROWS
    owned = jnp.where(owner == code_peer, 1.0, 0.0).astype(BF16)
    code = jnp.where(iota((LANES, docs), 0) == rank, (ids & (CLU_DEV - 1)) + 1, 0).astype(F32).astype(BF16)
    codes = lax.dot_general(owned, code, NT, preferred_element_type=F32).astype(BF16)
    out[peers, CAP * columns // LANES :, :] = codes.reshape(count, CODE_ROWS, LANES)


def prepare(ids_hbm, emb_ref, pos_ref, first_hbm, unit_hbm, emb, unit, first_ref, sems, ids_ref):
    docs, columns = emb.shape
    parts = 4
    size = docs // parts
    copies = [
        pltpu.make_async_copy(emb_ref.at[pl.ds(p * size, size)], emb.at[pl.ds(p * size, size)], sems.at[p])
        for p in range(parts)
    ]
    ids_copy = pltpu.make_async_copy(ids_hbm, ids_ref, sems.at[parts])
    ids_copy.start()
    for copy in copies:
        copy.start()
    ids_copy.wait()
    ids = ids_ref[...]
    rng = ids >> 2
    key = (ids * docs + iota(ids.shape, 1)).astype(F32)
    base = (rng * (CLU_DEV * docs)).astype(F32)
    key_col = jnp.transpose(jnp.broadcast_to(key, (LANES, docs)))
    ranks = []
    for lane in range(0, docs, LANES):
        before = (key_col < key[:, lane : lane + LANES]) & (key_col >= base[:, lane : lane + LANES])
        ranks.append(jnp.sum(jnp.where(before, 1.0, 0.0), axis=0, keepdims=True))
    rank = jnp.concatenate(ranks, axis=1).astype(jnp.int32)
    pos_ref[0:1, :] = rng
    pos_ref[1:2, :] = rank
    for p in range(parts):
        copies[p].wait()
        rows = emb[p * size : (p + 1) * size, :]
        scaling = lax.rsqrt(jnp.mean(rows * rows, axis=1, keepdims=True) + EPSILON) * columns ** (-0.5)
        unit[p * size : (p + 1) * size, :] = (rows * scaling).astype(BF16)
    unit_copy = pltpu.make_async_copy(unit, unit_hbm, sems.at[parts + 1])
    unit_copy.start()
    kind_rng = rng ^ (own_core() * PEERS)
    pos_ref[2:3, :] = kind_rng
    pos_ref[3:4, :] = ids
    out_copies = []
    for part in range(2):
        peers = slice(part * HALF, (part + 1) * HALF)
        place(unit[...], kind_rng, rank, ids, 0, first_ref, peers)
        out_copies.append(
            pltpu.make_async_copy(
                first_ref.at[pl.ds(part * HALF, HALF)], first_hbm.at[pl.ds(part * HALF, HALF)], sems.at[parts + 2 + part]
            )
        )
        out_copies[-1].start()
    unit_copy.wait()
    for copy in out_copies:
        copy.wait()


def place_other(pos_ref, unit_ref, out_ref):
    place(unit_ref[...], pos_ref[2:3, :], pos_ref[1:2, :], pos_ref[3:4, :], 1, out_ref, slice(0, PEERS))


def slot_codes(ref):
    codes = ref[:, ref.shape[1] - CODE_ROWS :, :].astype(F32)[:, 0, :].astype(BF16)
    lane = iota((1, ref.shape[0] * CAP), 1)
    spread = jnp.where(iota((CAP, lane.shape[1]), 0) == lane % CAP, 1.0, 0.0).astype(BF16)
    wide = lax.dot_general(codes[:, :CAP], spread, NN, preferred_element_type=F32)
    return jnp.sum(jnp.where(iota(wide.shape, 0) == lane // CAP, wide, 0.0), axis=0, keepdims=True)


def block_rows(ref, start, peers):
    tiles = (ref.shape[1] - CODE_ROWS) // CAP
    parts = [ref[start : start + peers, t * CAP : (t + 1) * CAP, :].reshape(peers * CAP, LANES) for t in range(tiles)]
    return jnp.concatenate(parts, axis=1)


def holder(names, block):
    return next(n for n in names if n[:2] == block[:2] and n[2] <= block[2] < n[2] + n[3])


def scores(names, new, loaded, pairs, fresh, last, best_in_ref, codes_in_ref, *refs):
    arrays = dict(zip(names, refs[: len(names)]))
    refs = list(refs[len(names) :])
    best_ref, codes_ref = refs[:2]
    copies = {}
    for number, name in enumerate(loaded):
        target = refs[2] if name == loaded[-1] else refs[3 + number]
        copies[name] = pltpu.make_async_copy(arrays[name], target, refs[-1].at[number])
        copies[name].start()
        arrays[name] = target
    if fresh:
        best_ref[...] = jnp.full(best_ref.shape, -1.0, F32)
        codes_ref[...] = jnp.zeros(codes_ref.shape, F32)
    else:
        best_ref[...] = best_in_ref[...]
        codes_ref[...] = codes_in_ref[...]

    def at(block):
        role, kind, start, peers = block
        return slice(role * 2 + kind, role * 2 + kind + 1), slice(start * CAP, (start + peers) * CAP)

    def rows_of(block):
        name = holder(names, block)
        return block_rows(arrays[name], block[2] - name[2], block[3])

    def arrive(name):
        if name in copies:
            copies.pop(name).wait()
        codes_ref[at(name)] = slot_codes(arrays[name])

    def into(block, values):
        best_ref[at(block)] = jnp.maximum(best_ref[at(block)], values)

    def run(some):
        for left in dict.fromkeys(p[0] for p in some):
            left_rows = rows_of(left)
            left_codes = codes_ref[at(left)]
            left_codes = jnp.where(left_codes > 0, left_codes, -1.0)
            left_codes = jnp.transpose(jnp.broadcast_to(left_codes, (LANES, left_codes.shape[1])))[:, :1]
            total = None
            for right in [p[1] for p in some if p[0] == left]:
                score = lax.dot_general(left_rows, rows_of(right), NT, preferred_element_type=F32)
                allowed = left_codes == codes_ref[at(right)]
                if left == right:
                    allowed = allowed & (iota(score.shape, 0) != iota(score.shape, 1))
                score = jnp.where(allowed, score, -1.0)
                into(right, jnp.max(score, axis=0, keepdims=True))
                if left != right:
                    for lane in range(0, score.shape[1], LANES):
                        part = score[:, lane : lane + LANES]
                        total = part if total is None else jnp.maximum(total, part)
            if total is not None:
                into(left, jnp.max(jnp.transpose(total), axis=0, keepdims=True))

    waiting = list(new)
    for some in pairs:
        for name in [n for n in waiting if any(holder(names, block) == n for p in some for block in p[:2])]:
            waiting.remove(name)
            arrive(name)
        run([p[:2] for p in some if p[2] == ALWAYS])
        for when in (HEAVY, LIGHT):
            part = [p[:2] for p in some if p[2] == when]
            if part:
                pl.when(((own_spot() + 1) & 2) == 2 * (1 - when))(functools.partial(run, part))
    if last:
        pack(best_ref, refs[2])


def pack(best_ref, out_ref):
    core, spot = own_core(), own_spot()
    out_ref[...] = jnp.full(out_ref.shape, -1.0, F32)
    for kind in range(2):
        from_core = core if kind == 0 else 1 - core
        for role, shift in ((OWN, 0), (NEAR, 1), (FAR, 3)):
            line = (spot + shift) % SIDE
            row = role * 2 + kind
            for peer in range(PEERS):
                first = peer * (2 * SIDE) + from_core * SIDE + line
                second = peer // SIDE * (2 * PEERS) + line * (2 * SIDE) + from_core * SIDE + peer % SIDE
                device = jnp.where(core == 0, first, second)
                out_ref[pl.ds(device, 1), :] = best_ref[row : row + 1, peer * CAP : (peer + 1) * CAP]


def finish(pos_ref, got_ref, out_ref):
    rng, rank = pos_ref[0:1, :], pos_ref[1:2, :]
    docs = rng.shape[1]
    first = got_ref[pl.ds(0, PEERS, stride=2 * SIDE), :]
    for line in range(1, SIDE):
        first = jnp.maximum(first, got_ref[pl.ds(line, PEERS, stride=2 * SIDE), :])
    second = []
    for z in range(SIDE):
        rows = [got_ref[pl.ds(z * 2 * PEERS + line * 2 * SIDE + SIDE, SIDE), :] for line in range(SIDE)]
        second.append(functools.reduce(jnp.maximum, rows))
    best = jnp.concatenate([first] + second, axis=0)
    pick = jnp.where(iota((best.shape[0], docs), 0) == rng, 1.0, 0.0)
    found = lax.dot_general(
        best, pick, (((0,), (0,)), ((), ())), precision=lax.Precision.HIGHEST, preferred_element_type=F32
    )
    out_ref[...] = jnp.sum(jnp.where(iota((CAP, docs), 0) == rank, found, 0.0), axis=0, keepdims=True)


def after(x, *others):
    return lax.optimization_barrier((x, *others))[0]


def per_device(embeddings, cluster_id):
    docs, columns = embeddings.shape
    devices = lax.axis_size("docs") * lax.axis_size("split")
    slots = jax.ShapeDtypeStruct((PEERS, CAP * columns // LANES + CODE_ROWS, LANES), BF16)

    pos, first, unit = pl.pallas_call(
        prepare,
        in_specs=[HBM, HBM],
        out_specs=[VMEM, HBM, HBM],
        out_shape=[
            jax.ShapeDtypeStruct((4, docs), jnp.int32),
            slots,
            jax.ShapeDtypeStruct((docs, columns), BF16),
        ],
        scratch_shapes=[
            pltpu.VMEM((docs, columns), F32),
            pltpu.VMEM((docs, columns), BF16),
            pltpu.VMEM(slots.shape, BF16),
            pltpu.SemaphoreType.DMA((8,)),
            pltpu.VMEM((1, docs), jnp.int32),
        ],
        compiler_params=PARAMS,
        name="prepare",
    )(pltpu.with_memory_space_constraint(cluster_id.reshape(1, docs), pltpu.HBM), pltpu.with_memory_space_constraint(embeddings, pltpu.HBM))

    other = pl.pallas_call(
        place_other,
        in_specs=[VMEM, VMEM],
        out_specs=VMEM,
        out_shape=slots,
        compiler_params=PARAMS,
        name="place_other",
    )(lax.ppermute(pos, AXES, core_moves()), lax.ppermute(unit, AXES, core_moves()))

    groups = plane_groups()
    moves_near = line_moves([(a, a - 1) for a in range(SIDE)])
    moves_far = line_moves([(a, a + 1) for a in range(SIDE)])

    def to_owner(x):
        return lax.all_to_all(x, AXES, 0, 0, axis_index_groups=groups, tiled=True)

    held = {}

    def score_call(state, new, pairs, name, loaded=(), last=False):
        names = sorted({holder(held, n) for some in pairs for p in some for n in p[:2]})
        table = jax.ShapeDtypeStruct((ROWS, PEERS * CAP), F32)
        extra = [jax.ShapeDtypeStruct(held[n].shape, BF16) for n in loaded[-1:]]
        if last:
            extra.append(jax.ShapeDtypeStruct((devices, CAP), F32))
        scratch = [pltpu.VMEM(held[n].shape, BF16) for n in loaded[:-1]]
        if loaded:
            scratch.append(pltpu.SemaphoreType.DMA((len(loaded),)))
        out = pl.pallas_call(
            lambda *refs: scores(names, new, loaded, pairs, state[0] is pos, last, *refs),
            in_specs=[VMEM, VMEM] + [HBM if n in loaded else VMEM for n in names],
            out_specs=[VMEM] * (2 + len(extra)),
            out_shape=[table, table, *extra],
            scratch_shapes=scratch,
            compiler_params=SCORE_PARAMS,
            name=name,
        )(*state[:2], *[held[n] for n in names])
        held.update(zip(loaded[-1:], out[2:]))
        return out

    def blocks(role, kind, start=0, end=PEERS):
        return [(role, kind, p, min(HALF, end - p)) for p in range(start, end, HALF)]

    def every(lefts, rights, when=ALWAYS):
        return [(a, b, when) for a in lefts for b in rights if a[:2] != b[:2] or a <= b]

    own_0, own_1, near_0, far_0 = blocks(OWN, 0), blocks(OWN, 1), blocks(NEAR, 0), blocks(FAR, 0)
    whole_0 = [(role, 0, 0, PEERS) for role in (OWN, NEAR, FAR)]
    own = to_owner(first)
    held[whole_0[0]] = own
    held[whole_0[1]] = lax.ppermute(own, AXES, moves_near)
    held[whole_0[2]] = lax.ppermute(own, AXES, moves_far)
    state = score_call((pos, pos), whole_0[:1], [every(own_0, own_0)], "scores_own_first")
    own = to_owner(other)
    whole_1 = (OWN, 1, 0, PEERS)
    held[whole_1] = own
    own = after(own, state[0])
    parts = ((0, 8), (8, 12), (12, 16))
    for start, end in parts:
        held[NEAR, 1, start, end - start] = lax.ppermute(own[start:end], AXES, moves_near)
        if not start:
            held[FAR, 1, 0, PEERS] = lax.ppermute(own, AXES, moves_far)
            state = score_call(state, (whole_1,), [every(own_0, own_1) + every(own_1, own_1)], "scores_own")
            own = after(own, state[0])
    state = score_call(
        state,
        whole_0[1:],
        [every(own_0 + own_1, near_0), every(near_0[:1], far_0, HEAVY) + every(near_0, far_0[1:], LIGHT)],
        "scores_near_first",
        whole_0[1:],
    )
    for start, end in parts:
        near = blocks(NEAR, 1, start, end)
        new = ((NEAR, 1, start, end - start),)
        pairs = [every(own_0 + own_1, near) + every(near, far_0)]
        if end == PEERS:
            new += ((FAR, 1, 0, PEERS),)
            older = [block for part in parts for block in blocks(NEAR, 1, *part)]
            far_1 = blocks(FAR, 1)
            first_half = [block for block in older if block[2] < HALF]
            pairs.append(every(first_half, far_1, HEAVY) + every(older, far_1[1:], LIGHT))
        state = score_call(state, new, pairs, f"scores_near_{start}", (), end == PEERS)
    got = lax.all_to_all(state[2], AXES, 0, 0, tiled=True)
    out = pl.pallas_call(
        finish,
        in_specs=[VMEM, VMEM],
        out_specs=VMEM,
        out_shape=jax.ShapeDtypeStruct((1, docs), F32),
        compiler_params=PARAMS,
        name="finish",
    )(pos, got)
    return out.reshape(docs)


def solution(mesh):
    return jax.shard_map(
        per_device,
        mesh=mesh,
        in_specs=(P(AXES, None), P(AXES)),
        out_specs=P(AXES),
        check_vma=False,
    )
```

```python
import functools

import jax
import jax.numpy as jnp
from jax import lax
from jax.experimental import pallas as pl
from jax.experimental.pallas import tpu as pltpu
from jax.sharding import PartitionSpec as P

F32 = jnp.float32
BF16 = jnp.bfloat16
CLU_DEV = 4
EPSILON = 1e-06
SIDE = 4
PEERS = SIDE * SIDE
CAP = 64
LANES = 128
CODE_ROWS = 8
HALF = PEERS // 2
ROWS = 8
CHUNKS = ((0, 0, 64), (1, 0, 48), (1, 48, 16))
BLOCKS = (((0, 32), (32, 32)), ((0, 32), (32, 16)), ((0, 16),))
OWN, NEAR, FAR = 0, 1, 2
LIGHT, HEAVY, ALWAYS = 0, 1, 2
AXES = ("docs", "split")
NT = (((1,), (1,)), ((), ()))
NN = (((1,), (0,)), ((), ()))
VMEM = pl.BlockSpec(memory_space=pltpu.VMEM)
HBM = pl.BlockSpec(memory_space=pltpu.HBM)
PARAMS = pltpu.CompilerParams(vmem_limit_bytes=24 * 2**20)
SCORE_PARAMS = pltpu.CompilerParams(vmem_limit_bytes=28 * 2**20)


def iota(shape, axis):
    return lax.broadcasted_iota(jnp.int32, shape, axis)


def flat(x, y, z, core):
    return ((z % SIDE * SIDE + y % SIDE) * 2 + core) * SIDE + x % SIDE


def plane_groups():
    side = range(SIDE)
    first = [[flat(x, y, z, 0) for z in side for y in side] for x in side]
    return first + [[flat(x, y, z, 1) for z in side for x in side] for y in side]


def line_moves(steps):
    side = range(SIDE)
    out = [(flat(a, u, z, 0), flat(b, u, z, 0)) for a, b in steps for u in side for z in side]
    return out + [(flat(u, a, z, 1), flat(u, b, z, 1)) for a, b in steps for u in side for z in side]


def core_moves():
    side = range(SIDE)
    return [(flat(x, y, z, c), flat(x, y, z, 1 - c)) for x in side for y in side for z in side for c in (0, 1)]


def own_core():
    return lax.axis_index("docs") & 1


def own_spot():
    return jnp.where(own_core() == 0, lax.axis_index("split"), (lax.axis_index("docs") >> 1) & (SIDE - 1))


def place(unit, kind_rng, rank, ids, kind, out, peers):
    docs, columns = unit.shape
    count = peers.stop - peers.start
    owner = kind_rng - (kind * PEERS + peers.start)
    inside = (owner >= 0) & (owner < count) & (rank < CAP)
    row = jnp.where(inside, owner * CAP + rank, -1)
    pick = jnp.where(iota((count * CAP, docs), 0) == row, 1.0, 0.0).astype(BF16)
    rows = lax.dot_general(pick, unit, NN, preferred_element_type=F32).astype(BF16)
    for tile in range(columns // LANES):
        part = rows[:, tile * LANES : (tile + 1) * LANES]
        out[peers, tile * CAP : (tile + 1) * CAP, :] = part.reshape(count, CAP, LANES)
    code_peer = iota((count * CODE_ROWS, docs), 0) // CODE_ROWS
    owned = jnp.where(owner == code_peer, 1.0, 0.0).astype(BF16)
    code = jnp.where(iota((LANES, docs), 0) == rank, (ids & (CLU_DEV - 1)) + 1, 0).astype(F32).astype(BF16)
    codes = lax.dot_general(owned, code, NT, preferred_element_type=F32).astype(BF16)
    out[peers, CAP * columns // LANES :, :] = codes.reshape(count, CODE_ROWS, LANES)


def prepare(ids_hbm, emb_ref, pos_ref, first_hbm, unit_hbm, emb, unit, first_ref, sems, ids_ref):
    docs, columns = emb.shape
    parts = 4
    size = docs // parts
    copies = [
        pltpu.make_async_copy(emb_ref.at[pl.ds(p * size, size)], emb.at[pl.ds(p * size, size)], sems.at[p])
        for p in range(parts)
    ]
    ids_copy = pltpu.make_async_copy(ids_hbm, ids_ref, sems.at[parts])
    ids_copy.start()
    for copy in copies:
        copy.start()
    ids_copy.wait()
    ids = ids_ref[...]
    rng = ids >> 2
    key = (ids * docs + iota(ids.shape, 1)).astype(F32)
    base = (rng * (CLU_DEV * docs)).astype(F32)
    key_col = jnp.transpose(jnp.broadcast_to(key, (LANES, docs)))
    ranks = []
    for lane in range(0, docs, LANES):
        before = (key_col < key[:, lane : lane + LANES]) & (key_col >= base[:, lane : lane + LANES])
        ranks.append(jnp.sum(jnp.where(before, 1.0, 0.0), axis=0, keepdims=True))
    rank = jnp.concatenate(ranks, axis=1).astype(jnp.int32)
    pos_ref[0:1, :] = rng
    pos_ref[1:2, :] = rank
    for p in range(parts):
        copies[p].wait()
        rows = emb[p * size : (p + 1) * size, :]
        scaling = lax.rsqrt(jnp.mean(rows * rows, axis=1, keepdims=True) + EPSILON) * columns ** (-0.5)
        unit[p * size : (p + 1) * size, :] = (rows * scaling).astype(BF16)
    unit_copy = pltpu.make_async_copy(unit, unit_hbm, sems.at[parts + 1])
    unit_copy.start()
    kind_rng = rng ^ (own_core() * PEERS)
    pos_ref[2:3, :] = kind_rng
    pos_ref[3:4, :] = ids
    out_copies = []
    for part in range(2):
        peers = slice(part * HALF, (part + 1) * HALF)
        place(unit[...], kind_rng, rank, ids, 0, first_ref, peers)
        out_copies.append(
            pltpu.make_async_copy(
                first_ref.at[pl.ds(part * HALF, HALF)], first_hbm.at[pl.ds(part * HALF, HALF)], sems.at[parts + 2 + part]
            )
        )
        out_copies[-1].start()
    unit_copy.wait()
    for copy in out_copies:
        copy.wait()


def place_other(pos_ref, unit_ref, out_ref):
    place(unit_ref[...], pos_ref[2:3, :], pos_ref[1:2, :], pos_ref[3:4, :], 1, out_ref, slice(0, PEERS))


def slot_codes(ref):
    codes = ref[:, ref.shape[1] - CODE_ROWS :, :].astype(F32)[:, 0, :].astype(BF16)
    lane = iota((1, ref.shape[0] * CAP), 1)
    spread = jnp.where(iota((CAP, lane.shape[1]), 0) == lane % CAP, 1.0, 0.0).astype(BF16)
    wide = lax.dot_general(codes[:, :CAP], spread, NN, preferred_element_type=F32)
    return jnp.sum(jnp.where(iota(wide.shape, 0) == lane // CAP, wide, 0.0), axis=0, keepdims=True)


def block_rows(ref, start, peers):
    tiles = (ref.shape[1] - CODE_ROWS) // CAP
    parts = [ref[start : start + peers, t * CAP : (t + 1) * CAP, :].reshape(peers * CAP, LANES) for t in range(tiles)]
    return jnp.concatenate(parts, axis=1)


def holder(names, block):
    return next(n for n in names if n[:2] == block[:2] and n[2] <= block[2] < n[2] + n[3])


def scores(names, new, loaded, pairs, fresh, last, best_in_ref, codes_in_ref, *refs):
    arrays = dict(zip(names, refs[: len(names)]))
    refs = list(refs[len(names) :])
    best_ref, codes_ref = refs[:2]
    copies = {}
    for number, name in enumerate(loaded):
        target = refs[2] if name == loaded[-1] else refs[3 + number]
        copies[name] = pltpu.make_async_copy(arrays[name], target, refs[-1].at[number])
        copies[name].start()
        arrays[name] = target
    if fresh:
        best_ref[...] = jnp.full(best_ref.shape, -1.0, F32)
        codes_ref[...] = jnp.zeros(codes_ref.shape, F32)
    else:
        best_ref[...] = best_in_ref[...]
        codes_ref[...] = codes_in_ref[...]

    def at(block):
        role, kind, start, peers = block
        return slice(role * 2 + kind, role * 2 + kind + 1), slice(start * CAP, (start + peers) * CAP)

    def rows_of(block):
        name = holder(names, block)
        return block_rows(arrays[name], block[2] - name[2], block[3])

    def arrive(name):
        if name in copies:
            copies.pop(name).wait()
        codes_ref[at(name)] = slot_codes(arrays[name])

    def into(block, values):
        best_ref[at(block)] = jnp.maximum(best_ref[at(block)], values)

    def run(some):
        for left in dict.fromkeys(p[0] for p in some):
            left_rows = rows_of(left)
            left_codes = codes_ref[at(left)]
            left_codes = jnp.where(left_codes > 0, left_codes, -1.0)
            left_codes = jnp.transpose(jnp.broadcast_to(left_codes, (LANES, left_codes.shape[1])))[:, :1]
            total = None
            for right in [p[1] for p in some if p[0] == left]:
                score = lax.dot_general(left_rows, rows_of(right), NT, preferred_element_type=F32)
                allowed = left_codes == codes_ref[at(right)]
                if left == right:
                    allowed = allowed & (iota(score.shape, 0) != iota(score.shape, 1))
                score = jnp.where(allowed, score, -1.0)
                into(right, jnp.max(score, axis=0, keepdims=True))
                if left != right:
                    for lane in range(0, score.shape[1], LANES):
                        part = score[:, lane : lane + LANES]
                        total = part if total is None else jnp.maximum(total, part)
            if total is not None:
                into(left, jnp.max(jnp.transpose(total), axis=0, keepdims=True))

    waiting = list(new)
    for some in pairs:
        for name in [n for n in waiting if any(holder(names, block) == n for p in some for block in p[:2])]:
            waiting.remove(name)
            arrive(name)
        run([p[:2] for p in some if p[2] == ALWAYS])
        for when in (HEAVY, LIGHT):
            part = [p[:2] for p in some if p[2] == when]
            if part:
                pl.when(((own_spot() + 1) & 2) == 2 * (1 - when))(functools.partial(run, part))
    if last:
        pack(best_ref, refs[2])


def pack(best_ref, out_ref):
    core, spot = own_core(), own_spot()
    out_ref[...] = jnp.full(out_ref.shape, -1.0, F32)
    for kind in range(2):
        from_core = core if kind == 0 else 1 - core
        for role, shift in ((OWN, 0), (NEAR, 1), (FAR, 3)):
            line = (spot + shift) % SIDE
            row = role * 2 + kind
            for peer in range(PEERS):
                first = peer * (2 * SIDE) + from_core * SIDE + line
                second = peer // SIDE * (2 * PEERS) + line * (2 * SIDE) + from_core * SIDE + peer % SIDE
                device = jnp.where(core == 0, first, second)
                out_ref[pl.ds(device, 1), :] = best_ref[row : row + 1, peer * CAP : (peer + 1) * CAP]


def finish(pos_ref, got_ref, out_ref):
    rng, rank = pos_ref[0:1, :], pos_ref[1:2, :]
    docs = rng.shape[1]
    first = got_ref[pl.ds(0, PEERS, stride=2 * SIDE), :]
    for line in range(1, SIDE):
        first = jnp.maximum(first, got_ref[pl.ds(line, PEERS, stride=2 * SIDE), :])
    second = []
    for z in range(SIDE):
        rows = [got_ref[pl.ds(z * 2 * PEERS + line * 2 * SIDE + SIDE, SIDE), :] for line in range(SIDE)]
        second.append(functools.reduce(jnp.maximum, rows))
    best = jnp.concatenate([first] + second, axis=0)
    pick = jnp.where(iota((best.shape[0], docs), 0) == rng, 1.0, 0.0)
    found = lax.dot_general(
        best, pick, (((0,), (0,)), ((), ())), precision=lax.Precision.HIGHEST, preferred_element_type=F32
    )
    out_ref[...] = jnp.sum(jnp.where(iota((CAP, docs), 0) == rank, found, 0.0), axis=0, keepdims=True)


def after(x, *others):
    return lax.optimization_barrier((x, *others))[0]


def per_device(embeddings, cluster_id):
    docs, columns = embeddings.shape
    devices = lax.axis_size("docs") * lax.axis_size("split")
    slots = jax.ShapeDtypeStruct((PEERS, CAP * columns // LANES + CODE_ROWS, LANES), BF16)

    pos, first, unit = pl.pallas_call(
        prepare,
        in_specs=[HBM, HBM],
        out_specs=[VMEM, HBM, HBM],
        out_shape=[
            jax.ShapeDtypeStruct((4, docs), jnp.int32),
            slots,
            jax.ShapeDtypeStruct((docs, columns), BF16),
        ],
        scratch_shapes=[
            pltpu.VMEM((docs, columns), F32),
            pltpu.VMEM((docs, columns), BF16),
            pltpu.VMEM(slots.shape, BF16),
            pltpu.SemaphoreType.DMA((8,)),
            pltpu.VMEM((1, docs), jnp.int32),
        ],
        compiler_params=PARAMS,
        name="prepare",
    )(pltpu.with_memory_space_constraint(cluster_id.reshape(1, docs), pltpu.HBM), pltpu.with_memory_space_constraint(embeddings, pltpu.HBM))

    other = pl.pallas_call(
        place_other,
        in_specs=[VMEM, VMEM],
        out_specs=VMEM,
        out_shape=slots,
        compiler_params=PARAMS,
        name="place_other",
    )(lax.ppermute(pos, AXES, core_moves()), lax.ppermute(unit, AXES, core_moves()))

    groups = plane_groups()
    moves_near = line_moves([(a, a - 1) for a in range(SIDE)])
    moves_far = line_moves([(a, a + 1) for a in range(SIDE)])

    def to_owner(x):
        return lax.all_to_all(x, AXES, 0, 0, axis_index_groups=groups, tiled=True)

    held = {}

    def score_call(state, new, pairs, name, loaded=(), last=False):
        names = sorted({holder(held, n) for some in pairs for p in some for n in p[:2]})
        table = jax.ShapeDtypeStruct((ROWS, PEERS * CAP), F32)
        extra = [jax.ShapeDtypeStruct(held[n].shape, BF16) for n in loaded[-1:]]
        if last:
            extra.append(jax.ShapeDtypeStruct((devices, CAP), F32))
        scratch = [pltpu.VMEM(held[n].shape, BF16) for n in loaded[:-1]]
        if loaded:
            scratch.append(pltpu.SemaphoreType.DMA((len(loaded),)))
        out = pl.pallas_call(
            lambda *refs: scores(names, new, loaded, pairs, state[0] is pos, last, *refs),
            in_specs=[VMEM, VMEM] + [HBM if n in loaded else VMEM for n in names],
            out_specs=[VMEM] * (2 + len(extra)),
            out_shape=[table, table, *extra],
            scratch_shapes=scratch,
            compiler_params=SCORE_PARAMS,
            name=name,
        )(*state[:2], *[held[n] for n in names])
        held.update(zip(loaded[-1:], out[2:]))
        return out

    def blocks(role, kind, start=0, end=PEERS):
        return [(role, kind, p, min(HALF, end - p)) for p in range(start, end, HALF)]

    def every(lefts, rights, when=ALWAYS):
        return [(a, b, when) for a in lefts for b in rights if a[:2] != b[:2] or a <= b]

    own_0, own_1, near_0, far_0 = blocks(OWN, 0), blocks(OWN, 1), blocks(NEAR, 0), blocks(FAR, 0)
    whole_0 = [(role, 0, 0, PEERS) for role in (OWN, NEAR, FAR)]
    own = to_owner(first)
    held[whole_0[0]] = own
    held[whole_0[1]] = lax.ppermute(own, AXES, moves_near)
    held[whole_0[2]] = lax.ppermute(own, AXES, moves_far)
    state = score_call((pos, pos), whole_0[:1], [every(own_0, own_0)], "scores_own_first")
    own = to_owner(other)
    whole_1 = (OWN, 1, 0, PEERS)
    held[whole_1] = own
    own = after(own, state[0])
    parts = ((0, 8), (8, 12), (12, 16))
    for start, end in parts:
        held[NEAR, 1, start, end - start] = lax.ppermute(own[start:end], AXES, moves_near)
        if not start:
            held[FAR, 1, 0, PEERS] = lax.ppermute(own, AXES, moves_far)
            state = score_call(state, (whole_1,), [every(own_0, own_1) + every(own_1, own_1)], "scores_own")
            own = after(own, state[0])
    state = score_call(
        state,
        whole_0[1:],
        [every(own_0 + own_1, near_0), every(near_0[:1], far_0, HEAVY) + every(near_0, far_0[1:], LIGHT)],
        "scores_near_first",
        whole_0[1:],
    )
    for start, end in parts:
        near = blocks(NEAR, 1, start, end)
        new = ((NEAR, 1, start, end - start),)
        pairs = [every(own_0 + own_1, near) + every(near, far_0)]
        if end == PEERS:
            new += ((FAR, 1, 0, PEERS),)
            older = [block for part in parts for block in blocks(NEAR, 1, *part)]
            far_1 = blocks(FAR, 1)
            first_half = [block for block in older if block[2] < HALF]
            pairs.append(every(first_half, far_1, HEAVY) + every(older, far_1[1:], LIGHT))
        state = score_call(state, new, pairs, f"scores_near_{start}", (), end == PEERS)
    got = lax.all_to_all(state[2], AXES, 0, 0, tiled=True)
    out = pl.pallas_call(
        finish,
        in_specs=[VMEM, VMEM],
        out_specs=VMEM,
        out_shape=jax.ShapeDtypeStruct((1, docs), F32),
        compiler_params=PARAMS,
        name="finish",
    )(pos, got)
    return out.reshape(docs)


def solution(mesh):
    return jax.shard_map(
        per_device,
        mesh=mesh,
        in_specs=(P(AXES, None), P(AXES)),
        out_specs=P(AXES),
        check_vma=False,
    )
```

```python
import functools

import jax
import jax.numpy as jnp
from jax import lax
from jax.experimental import pallas as pl
from jax.experimental.pallas import tpu as pltpu
from jax.sharding import PartitionSpec as P

F32 = jnp.float32
BF16 = jnp.bfloat16
CLU_DEV = 4
EPSILON = 1e-06
SIDE = 4
PEERS = SIDE * SIDE
CAP = 64
LANES = 128
CODE_ROWS = 8
HALF = PEERS // 2
ROWS = 8
CHUNKS = ((0, 0, 64), (1, 0, 48), (1, 48, 16))
BLOCKS = (((0, 32), (32, 32)), ((0, 32), (32, 16)), ((0, 16),))
OWN, NEAR, FAR = 0, 1, 2
LIGHT, HEAVY, ALWAYS = 0, 1, 2
AXES = ("docs", "split")
NT = (((1,), (1,)), ((), ()))
NN = (((1,), (0,)), ((), ()))
VMEM = pl.BlockSpec(memory_space=pltpu.VMEM)
HBM = pl.BlockSpec(memory_space=pltpu.HBM)
PARAMS = pltpu.CompilerParams(vmem_limit_bytes=24 * 2**20)
SCORE_PARAMS = pltpu.CompilerParams(vmem_limit_bytes=28 * 2**20)


def iota(shape, axis):
    return lax.broadcasted_iota(jnp.int32, shape, axis)


def flat(x, y, z, core):
    return ((z % SIDE * SIDE + y % SIDE) * 2 + core) * SIDE + x % SIDE


def plane_groups():
    side = range(SIDE)
    first = [[flat(x, y, z, 0) for z in side for y in side] for x in side]
    return first + [[flat(x, y, z, 1) for z in side for x in side] for y in side]


def line_moves(steps):
    side = range(SIDE)
    out = [(flat(a, u, z, 0), flat(b, u, z, 0)) for a, b in steps for u in side for z in side]
    return out + [(flat(u, a, z, 1), flat(u, b, z, 1)) for a, b in steps for u in side for z in side]


def core_moves():
    side = range(SIDE)
    return [(flat(x, y, z, c), flat(x, y, z, 1 - c)) for x in side for y in side for z in side for c in (0, 1)]


def own_core():
    return lax.axis_index("docs") & 1


def own_spot():
    return jnp.where(own_core() == 0, lax.axis_index("split"), (lax.axis_index("docs") >> 1) & (SIDE - 1))


def place(unit, kind_rng, rank, ids, kind, out, peers):
    docs, columns = unit.shape
    count = peers.stop - peers.start
    owner = kind_rng - (kind * PEERS + peers.start)
    inside = (owner >= 0) & (owner < count) & (rank < CAP)
    row = jnp.where(inside, owner * CAP + rank, -1)
    pick = jnp.where(iota((count * CAP, docs), 0) == row, 1.0, 0.0).astype(BF16)
    rows = lax.dot_general(pick, unit, NN, preferred_element_type=F32).astype(BF16)
    for tile in range(columns // LANES):
        part = rows[:, tile * LANES : (tile + 1) * LANES]
        out[peers, tile * CAP : (tile + 1) * CAP, :] = part.reshape(count, CAP, LANES)
    code_peer = iota((count * CODE_ROWS, docs), 0) // CODE_ROWS
    owned = jnp.where(owner == code_peer, 1.0, 0.0).astype(BF16)
    code = jnp.where(iota((LANES, docs), 0) == rank, (ids & (CLU_DEV - 1)) + 1, 0).astype(F32).astype(BF16)
    codes = lax.dot_general(owned, code, NT, preferred_element_type=F32).astype(BF16)
    out[peers, CAP * columns // LANES :, :] = codes.reshape(count, CODE_ROWS, LANES)


def prepare(ids_hbm, emb_ref, pos_ref, first_hbm, unit_hbm, emb, unit, first_ref, sems, ids_ref):
    docs, columns = emb.shape
    parts = 4
    size = docs // parts
    copies = [
        pltpu.make_async_copy(emb_ref.at[pl.ds(p * size, size)], emb.at[pl.ds(p * size, size)], sems.at[p])
        for p in range(parts)
    ]
    ids_copy = pltpu.make_async_copy(ids_hbm, ids_ref, sems.at[parts])
    ids_copy.start()
    for copy in copies:
        copy.start()
    ids_copy.wait()
    ids = ids_ref[...]
    rng = ids >> 2
    key = (ids * docs + iota(ids.shape, 1)).astype(F32)
    base = (rng * (CLU_DEV * docs)).astype(F32)
    key_col = jnp.transpose(jnp.broadcast_to(key, (LANES, docs)))
    ranks = []
    for lane in range(0, docs, LANES):
        before = (key_col < key[:, lane : lane + LANES]) & (key_col >= base[:, lane : lane + LANES])
        ranks.append(jnp.sum(jnp.where(before, 1.0, 0.0), axis=0, keepdims=True))
    rank = jnp.concatenate(ranks, axis=1).astype(jnp.int32)
    pos_ref[0:1, :] = rng
    pos_ref[1:2, :] = rank
    for p in range(parts):
        copies[p].wait()
        rows = emb[p * size : (p + 1) * size, :]
        scaling = lax.rsqrt(jnp.mean(rows * rows, axis=1, keepdims=True) + EPSILON) * columns ** (-0.5)
        unit[p * size : (p + 1) * size, :] = (rows * scaling).astype(BF16)
    unit_copy = pltpu.make_async_copy(unit, unit_hbm, sems.at[parts + 1])
    unit_copy.start()
    kind_rng = rng ^ (own_core() * PEERS)
    pos_ref[2:3, :] = kind_rng
    pos_ref[3:4, :] = ids
    out_copies = []
    for part in range(2):
        peers = slice(part * HALF, (part + 1) * HALF)
        place(unit[...], kind_rng, rank, ids, 0, first_ref, peers)
        out_copies.append(
            pltpu.make_async_copy(
                first_ref.at[pl.ds(part * HALF, HALF)], first_hbm.at[pl.ds(part * HALF, HALF)], sems.at[parts + 2 + part]
            )
        )
        out_copies[-1].start()
    unit_copy.wait()
    for copy in out_copies:
        copy.wait()


def place_other(pos_ref, unit_ref, out_ref):
    place(unit_ref[...], pos_ref[2:3, :], pos_ref[1:2, :], pos_ref[3:4, :], 1, out_ref, slice(0, PEERS))


def slot_codes(ref):
    codes = ref[:, ref.shape[1] - CODE_ROWS :, :].astype(F32)[:, 0, :].astype(BF16)
    lane = iota((1, ref.shape[0] * CAP), 1)
    spread = jnp.where(iota((CAP, lane.shape[1]), 0) == lane % CAP, 1.0, 0.0).astype(BF16)
    wide = lax.dot_general(codes[:, :CAP], spread, NN, preferred_element_type=F32)
    return jnp.sum(jnp.where(iota(wide.shape, 0) == lane // CAP, wide, 0.0), axis=0, keepdims=True)


def block_rows(ref, start, peers):
    tiles = (ref.shape[1] - CODE_ROWS) // CAP
    parts = [ref[start : start + peers, t * CAP : (t + 1) * CAP, :].reshape(peers * CAP, LANES) for t in range(tiles)]
    return jnp.concatenate(parts, axis=1)


def holder(names, block):
    return next(n for n in names if n[:2] == block[:2] and n[2] <= block[2] < n[2] + n[3])


def scores(names, new, loaded, pairs, fresh, last, best_in_ref, codes_in_ref, *refs):
    arrays = dict(zip(names, refs[: len(names)]))
    refs = list(refs[len(names) :])
    best_ref, codes_ref = refs[:2]
    copies = {}
    for number, name in enumerate(loaded):
        target = refs[2] if name == loaded[-1] else refs[3 + number]
        copies[name] = pltpu.make_async_copy(arrays[name], target, refs[-1].at[number])
        copies[name].start()
        arrays[name] = target
    if fresh:
        best_ref[...] = jnp.full(best_ref.shape, -1.0, F32)
        codes_ref[...] = jnp.zeros(codes_ref.shape, F32)
    else:
        best_ref[...] = best_in_ref[...]
        codes_ref[...] = codes_in_ref[...]

    def at(block):
        role, kind, start, peers = block
        return slice(role * 2 + kind, role * 2 + kind + 1), slice(start * CAP, (start + peers) * CAP)

    def rows_of(block):
        name = holder(names, block)
        return block_rows(arrays[name], block[2] - name[2], block[3])

    def arrive(name):
        if name in copies:
            copies.pop(name).wait()
        codes_ref[at(name)] = slot_codes(arrays[name])

    def into(block, values):
        best_ref[at(block)] = jnp.maximum(best_ref[at(block)], values)

    def run(some):
        for left in dict.fromkeys(p[0] for p in some):
            left_rows = rows_of(left)
            left_codes = codes_ref[at(left)]
            left_codes = jnp.where(left_codes > 0, left_codes, -1.0)
            left_codes = jnp.transpose(jnp.broadcast_to(left_codes, (LANES, left_codes.shape[1])))[:, :1]
            total = None
            for right in [p[1] for p in some if p[0] == left]:
                score = lax.dot_general(left_rows, rows_of(right), NT, preferred_element_type=F32)
                allowed = left_codes == codes_ref[at(right)]
                if left == right:
                    allowed = allowed & (iota(score.shape, 0) != iota(score.shape, 1))
                score = jnp.where(allowed, score, -1.0)
                into(right, jnp.max(score, axis=0, keepdims=True))
                if left != right:
                    for lane in range(0, score.shape[1], LANES):
                        part = score[:, lane : lane + LANES]
                        total = part if total is None else jnp.maximum(total, part)
            if total is not None:
                into(left, jnp.max(jnp.transpose(total), axis=0, keepdims=True))

    waiting = list(new)
    for some in pairs:
        for name in [n for n in waiting if any(holder(names, block) == n for p in some for block in p[:2])]:
            waiting.remove(name)
            arrive(name)
        run([p[:2] for p in some if p[2] == ALWAYS])
        for when in (HEAVY, LIGHT):
            part = [p[:2] for p in some if p[2] == when]
            if part:
                pl.when(((own_spot() + 1) & 2) == 2 * (1 - when))(functools.partial(run, part))
    if last:
        pack(best_ref, refs[2])


def pack(best_ref, out_ref):
    core, spot = own_core(), own_spot()
    out_ref[...] = jnp.full(out_ref.shape, -1.0, F32)
    for kind in range(2):
        from_core = core if kind == 0 else 1 - core
        for role, shift in ((OWN, 0), (NEAR, 1), (FAR, 3)):
            line = (spot + shift) % SIDE
            row = role * 2 + kind
            for peer in range(PEERS):
                first = peer * (2 * SIDE) + from_core * SIDE + line
                second = peer // SIDE * (2 * PEERS) + line * (2 * SIDE) + from_core * SIDE + peer % SIDE
                device = jnp.where(core == 0, first, second)
                out_ref[pl.ds(device, 1), :] = best_ref[row : row + 1, peer * CAP : (peer + 1) * CAP]


def finish(pos_ref, got_ref, out_ref):
    rng, rank = pos_ref[0:1, :], pos_ref[1:2, :]
    docs = rng.shape[1]
    first = got_ref[pl.ds(0, PEERS, stride=2 * SIDE), :]
    for line in range(1, SIDE):
        first = jnp.maximum(first, got_ref[pl.ds(line, PEERS, stride=2 * SIDE), :])
    second = []
    for z in range(SIDE):
        rows = [got_ref[pl.ds(z * 2 * PEERS + line * 2 * SIDE + SIDE, SIDE), :] for line in range(SIDE)]
        second.append(functools.reduce(jnp.maximum, rows))
    best = jnp.concatenate([first] + second, axis=0)
    pick = jnp.where(iota((best.shape[0], docs), 0) == rng, 1.0, 0.0)
    found = lax.dot_general(
        best, pick, (((0,), (0,)), ((), ())), precision=lax.Precision.HIGHEST, preferred_element_type=F32
    )
    out_ref[...] = jnp.sum(jnp.where(iota((CAP, docs), 0) == rank, found, 0.0), axis=0, keepdims=True)


def after(x, *others):
    return lax.optimization_barrier((x, *others))[0]


def per_device(embeddings, cluster_id):
    docs, columns = embeddings.shape
    devices = lax.axis_size("docs") * lax.axis_size("split")
    slots = jax.ShapeDtypeStruct((PEERS, CAP * columns // LANES + CODE_ROWS, LANES), BF16)

    pos, first, unit = pl.pallas_call(
        prepare,
        in_specs=[HBM, HBM],
        out_specs=[VMEM, HBM, HBM],
        out_shape=[
            jax.ShapeDtypeStruct((4, docs), jnp.int32),
            slots,
            jax.ShapeDtypeStruct((docs, columns), BF16),
        ],
        scratch_shapes=[
            pltpu.VMEM((docs, columns), F32),
            pltpu.VMEM((docs, columns), BF16),
            pltpu.VMEM(slots.shape, BF16),
            pltpu.SemaphoreType.DMA((8,)),
            pltpu.VMEM((1, docs), jnp.int32),
        ],
        compiler_params=PARAMS,
        name="prepare",
    )(pltpu.with_memory_space_constraint(cluster_id.reshape(1, docs), pltpu.HBM), pltpu.with_memory_space_constraint(embeddings, pltpu.HBM))

    other = pl.pallas_call(
        place_other,
        in_specs=[VMEM, VMEM],
        out_specs=VMEM,
        out_shape=slots,
        compiler_params=PARAMS,
        name="place_other",
    )(lax.ppermute(pos, AXES, core_moves()), lax.ppermute(unit, AXES, core_moves()))

    groups = plane_groups()
    moves_near = line_moves([(a, a - 1) for a in range(SIDE)])
    moves_far = line_moves([(a, a + 1) for a in range(SIDE)])

    def to_owner(x):
        return lax.all_to_all(x, AXES, 0, 0, axis_index_groups=groups, tiled=True)

    held = {}

    def score_call(state, new, pairs, name, loaded=(), last=False):
        names = sorted({holder(held, n) for some in pairs for p in some for n in p[:2]})
        table = jax.ShapeDtypeStruct((ROWS, PEERS * CAP), F32)
        extra = [jax.ShapeDtypeStruct(held[n].shape, BF16) for n in loaded[-1:]]
        if last:
            extra.append(jax.ShapeDtypeStruct((devices, CAP), F32))
        scratch = [pltpu.VMEM(held[n].shape, BF16) for n in loaded[:-1]]
        if loaded:
            scratch.append(pltpu.SemaphoreType.DMA((len(loaded),)))
        out = pl.pallas_call(
            lambda *refs: scores(names, new, loaded, pairs, state[0] is pos, last, *refs),
            in_specs=[VMEM, VMEM] + [HBM if n in loaded else VMEM for n in names],
            out_specs=[VMEM] * (2 + len(extra)),
            out_shape=[table, table, *extra],
            scratch_shapes=scratch,
            compiler_params=SCORE_PARAMS,
            name=name,
        )(*state[:2], *[held[n] for n in names])
        held.update(zip(loaded[-1:], out[2:]))
        return out

    def blocks(role, kind, start=0, end=PEERS):
        return [(role, kind, p, min(HALF, end - p)) for p in range(start, end, HALF)]

    def every(lefts, rights, when=ALWAYS):
        return [(a, b, when) for a in lefts for b in rights if a[:2] != b[:2] or a <= b]

    own_0, own_1, near_0, far_0 = blocks(OWN, 0), blocks(OWN, 1), blocks(NEAR, 0), blocks(FAR, 0)
    whole_0 = [(role, 0, 0, PEERS) for role in (OWN, NEAR, FAR)]
    own = to_owner(first)
    held[whole_0[0]] = own
    held[whole_0[1]] = lax.ppermute(own, AXES, moves_near)
    held[whole_0[2]] = lax.ppermute(own, AXES, moves_far)
    state = score_call((pos, pos), whole_0[:1], [every(own_0, own_0)], "scores_own_first")
    own = to_owner(other)
    whole_1 = (OWN, 1, 0, PEERS)
    held[whole_1] = own
    own = after(own, state[0])
    parts = ((0, 12), (12, 16))
    for number, (start, end) in enumerate(parts):
        held[NEAR, 1, start, end - start] = lax.ppermute(own[start:end], AXES, moves_near)
        half = (1 - number) * HALF
        held[FAR, 1, half, HALF] = lax.ppermute(own[half : half + HALF], AXES, moves_far)
        if not start:
            state = score_call(state, (whole_1,), [every(own_0, own_1) + every(own_1, own_1)], "scores_own")
            own = after(own, state[0])
    state = score_call(
        state,
        whole_0[1:],
        [
            every(own_0 + own_1, near_0),
            every(own_1, far_0) + every(near_0[:1], far_0, HEAVY) + every(near_0, far_0[1:], LIGHT),
        ],
        "scores_near_first",
        whole_0[1:],
    )
    older, (far_a, far_b) = [], blocks(FAR, 1)
    for number, (start, end) in enumerate(parts):
        near = blocks(NEAR, 1, start, end)
        older += near
        new = ((NEAR, 1, start, end - start),)
        pairs = every(own_1, near) + every(near, far_0)
        if not start:
            new += (far_b,)
            pairs += every([b for b in older if b[2] < HALF], [far_b], HEAVY) + every(older, [far_b], LIGHT)
        else:
            new += (far_a,)
            pairs += every([b for b in older if b[2] < HALF], [far_a], HEAVY) + every(near, [far_b], LIGHT)
        state = score_call(state, new, [pairs], f"scores_near_{start}", last=end == PEERS)
    got = lax.all_to_all(state[2], AXES, 0, 0, tiled=True)
    out = pl.pallas_call(
        finish,
        in_specs=[VMEM, VMEM],
        out_specs=VMEM,
        out_shape=jax.ShapeDtypeStruct((1, docs), F32),
        compiler_params=PARAMS,
        name="finish",
    )(pos, got)
    return out.reshape(docs)


def solution(mesh):
    return jax.shard_map(
        per_device,
        mesh=mesh,
        in_specs=(P(AXES, None), P(AXES)),
        out_specs=P(AXES),
        check_vma=False,
    )
```

```python
import functools

import jax
import jax.numpy as jnp
from jax import lax
from jax.experimental import pallas as pl
from jax.experimental.pallas import tpu as pltpu
from jax.sharding import PartitionSpec as P

F32 = jnp.float32
BF16 = jnp.bfloat16
CLU_DEV = 4
EPSILON = 1e-06
SIDE = 4
PEERS = SIDE * SIDE
CAP = 64
LANES = 128
CODE_ROWS = 8
HALF = PEERS // 2
ROWS = 8
CHUNKS = ((0, 0, 64), (1, 0, 48), (1, 48, 16))
BLOCKS = (((0, 32), (32, 32)), ((0, 32), (32, 16)), ((0, 16),))
OWN, NEAR, FAR = 0, 1, 2
LIGHT, HEAVY, ALWAYS = 0, 1, 2
AXES = ("docs", "split")
NT = (((1,), (1,)), ((), ()))
NN = (((1,), (0,)), ((), ()))
VMEM = pl.BlockSpec(memory_space=pltpu.VMEM)
HBM = pl.BlockSpec(memory_space=pltpu.HBM)
PARAMS = pltpu.CompilerParams(vmem_limit_bytes=24 * 2**20)
SCORE_PARAMS = pltpu.CompilerParams(vmem_limit_bytes=28 * 2**20)


def iota(shape, axis):
    return lax.broadcasted_iota(jnp.int32, shape, axis)


def flat(x, y, z, core):
    return ((z % SIDE * SIDE + y % SIDE) * 2 + core) * SIDE + x % SIDE


def plane_groups():
    side = range(SIDE)
    first = [[flat(x, y, z, 0) for z in side for y in side] for x in side]
    return first + [[flat(x, y, z, 1) for z in side for x in side] for y in side]


def line_moves(steps):
    side = range(SIDE)
    out = [(flat(a, u, z, 0), flat(b, u, z, 0)) for a, b in steps for u in side for z in side]
    return out + [(flat(u, a, z, 1), flat(u, b, z, 1)) for a, b in steps for u in side for z in side]


def core_moves():
    side = range(SIDE)
    return [(flat(x, y, z, c), flat(x, y, z, 1 - c)) for x in side for y in side for z in side for c in (0, 1)]


def own_core():
    return lax.axis_index("docs") & 1


def own_spot():
    return jnp.where(own_core() == 0, lax.axis_index("split"), (lax.axis_index("docs") >> 1) & (SIDE - 1))


def place(unit, kind_rng, rank, ids, kind, out, peers):
    docs, columns = unit.shape
    count = peers.stop - peers.start
    owner = kind_rng - (kind * PEERS + peers.start)
    inside = (owner >= 0) & (owner < count) & (rank < CAP)
    row = jnp.where(inside, owner * CAP + rank, -1)
    pick = jnp.where(iota((count * CAP, docs), 0) == row, 1.0, 0.0).astype(BF16)
    rows = lax.dot_general(pick, unit, NN, preferred_element_type=F32).astype(BF16)
    for tile in range(columns // LANES):
        part = rows[:, tile * LANES : (tile + 1) * LANES]
        out[peers, tile * CAP : (tile + 1) * CAP, :] = part.reshape(count, CAP, LANES)
    code_peer = iota((count * CODE_ROWS, docs), 0) // CODE_ROWS
    owned = jnp.where(owner == code_peer, 1.0, 0.0).astype(BF16)
    code = jnp.where(iota((LANES, docs), 0) == rank, (ids & (CLU_DEV - 1)) + 1, 0).astype(F32).astype(BF16)
    codes = lax.dot_general(owned, code, NT, preferred_element_type=F32).astype(BF16)
    out[peers, CAP * columns // LANES :, :] = codes.reshape(count, CODE_ROWS, LANES)


def prepare(ids_hbm, emb_ref, pos_ref, first_hbm, unit_hbm, emb, unit, first_ref, sems, ids_ref):
    docs, columns = emb.shape
    parts = 4
    size = docs // parts
    copies = [
        pltpu.make_async_copy(emb_ref.at[pl.ds(p * size, size)], emb.at[pl.ds(p * size, size)], sems.at[p])
        for p in range(parts)
    ]
    ids_copy = pltpu.make_async_copy(ids_hbm, ids_ref, sems.at[parts])
    ids_copy.start()
    for copy in copies:
        copy.start()
    ids_copy.wait()
    ids = ids_ref[...]
    rng = ids >> 2
    key = (ids * docs + iota(ids.shape, 1)).astype(F32)
    base = (rng * (CLU_DEV * docs)).astype(F32)
    key_col = jnp.transpose(jnp.broadcast_to(key, (LANES, docs)))
    ranks = []
    for lane in range(0, docs, LANES):
        before = (key_col < key[:, lane : lane + LANES]) & (key_col >= base[:, lane : lane + LANES])
        ranks.append(jnp.sum(jnp.where(before, 1.0, 0.0), axis=0, keepdims=True))
    rank = jnp.concatenate(ranks, axis=1).astype(jnp.int32)
    pos_ref[0:1, :] = rng
    pos_ref[1:2, :] = rank
    for p in range(parts):
        copies[p].wait()
        rows = emb[p * size : (p + 1) * size, :]
        scaling = lax.rsqrt(jnp.mean(rows * rows, axis=1, keepdims=True) + EPSILON) * columns ** (-0.5)
        unit[p * size : (p + 1) * size, :] = (rows * scaling).astype(BF16)
    unit_copy = pltpu.make_async_copy(unit, unit_hbm, sems.at[parts + 1])
    unit_copy.start()
    kind_rng = rng ^ (own_core() * PEERS)
    pos_ref[2:3, :] = kind_rng
    pos_ref[3:4, :] = ids
    out_copies = []
    for part in range(2):
        peers = slice(part * HALF, (part + 1) * HALF)
        place(unit[...], kind_rng, rank, ids, 0, first_ref, peers)
        out_copies.append(
            pltpu.make_async_copy(
                first_ref.at[pl.ds(part * HALF, HALF)], first_hbm.at[pl.ds(part * HALF, HALF)], sems.at[parts + 2 + part]
            )
        )
        out_copies[-1].start()
    unit_copy.wait()
    for copy in out_copies:
        copy.wait()


def place_other(pos_ref, unit_ref, out_ref):
    place(unit_ref[...], pos_ref[2:3, :], pos_ref[1:2, :], pos_ref[3:4, :], 1, out_ref, slice(0, PEERS))


def slot_codes(ref):
    codes = ref[:, ref.shape[1] - CODE_ROWS :, :].astype(F32)[:, 0, :].astype(BF16)
    lane = iota((1, ref.shape[0] * CAP), 1)
    spread = jnp.where(iota((CAP, lane.shape[1]), 0) == lane % CAP, 1.0, 0.0).astype(BF16)
    wide = lax.dot_general(codes[:, :CAP], spread, NN, preferred_element_type=F32)
    return jnp.sum(jnp.where(iota(wide.shape, 0) == lane // CAP, wide, 0.0), axis=0, keepdims=True)


def block_rows(ref, start, peers):
    tiles = (ref.shape[1] - CODE_ROWS) // CAP
    parts = [ref[start : start + peers, t * CAP : (t + 1) * CAP, :].reshape(peers * CAP, LANES) for t in range(tiles)]
    return jnp.concatenate(parts, axis=1)


def holder(names, block):
    return next(n for n in names if n[:2] == block[:2] and n[2] <= block[2] < n[2] + n[3])


def scores(names, new, loaded, pairs, fresh, last, best_in_ref, codes_in_ref, *refs):
    arrays = dict(zip(names, refs[: len(names)]))
    refs = list(refs[len(names) :])
    if last:
        refs = [*refs[1:3], refs[0]]
    best_ref, codes_ref = refs[:2]
    copies = {}
    for number, name in enumerate(loaded):
        target = refs[2] if name == loaded[-1] else refs[3 + number]
        copies[name] = pltpu.make_async_copy(arrays[name], target, refs[-1].at[number])
        copies[name].start()
        arrays[name] = target
    if fresh:
        best_ref[...] = jnp.full(best_ref.shape, -1.0, F32)
        codes_ref[...] = jnp.zeros(codes_ref.shape, F32)
    else:
        best_ref[...] = best_in_ref[...]
        codes_ref[...] = codes_in_ref[...]

    def at(block):
        role, kind, start, peers = block
        return slice(role * 2 + kind, role * 2 + kind + 1), slice(start * CAP, (start + peers) * CAP)

    def rows_of(block):
        name = holder(names, block)
        return block_rows(arrays[name], block[2] - name[2], block[3])

    def arrive(name):
        if name in copies:
            copies.pop(name).wait()
        codes_ref[at(name)] = slot_codes(arrays[name])

    def into(block, values):
        best_ref[at(block)] = jnp.maximum(best_ref[at(block)], values)

    def run(some):
        for left in dict.fromkeys(p[0] for p in some):
            left_rows = rows_of(left)
            left_codes = codes_ref[at(left)]
            left_codes = jnp.where(left_codes > 0, left_codes, -1.0)
            left_codes = jnp.transpose(jnp.broadcast_to(left_codes, (LANES, left_codes.shape[1])))[:, :1]
            total = None
            for right in [p[1] for p in some if p[0] == left]:
                score = lax.dot_general(left_rows, rows_of(right), NT, preferred_element_type=F32)
                allowed = left_codes == codes_ref[at(right)]
                if left == right:
                    allowed = allowed & (iota(score.shape, 0) != iota(score.shape, 1))
                score = jnp.where(allowed, score, -1.0)
                into(right, jnp.max(score, axis=0, keepdims=True))
                if left != right:
                    for lane in range(0, score.shape[1], LANES):
                        part = score[:, lane : lane + LANES]
                        total = part if total is None else jnp.maximum(total, part)
            if total is not None:
                into(left, jnp.max(jnp.transpose(total), axis=0, keepdims=True))

    waiting = list(new)
    for some in pairs:
        for name in [n for n in waiting if any(holder(names, block) == n for p in some for block in p[:2])]:
            waiting.remove(name)
            arrive(name)
        run([p[:2] for p in some if p[2] == ALWAYS])
        for when in (HEAVY, LIGHT):
            part = [p[:2] for p in some if p[2] == when]
            if part:
                pl.when(((own_spot() + 1) & 2) == 2 * (1 - when))(functools.partial(run, part))
    if last:
        pack(best_ref, refs[2])


def pack(best_ref, out_ref):
    core, spot = own_core(), own_spot()
    out_ref[...] = jnp.full(out_ref.shape, -1.0, F32)
    for kind in range(2):
        from_core = core if kind == 0 else 1 - core
        for role, shift in ((OWN, 0), (NEAR, 1), (FAR, 3)):
            line = (spot + shift) % SIDE
            row = role * 2 + kind
            for peer in range(PEERS):
                first = peer * (2 * SIDE) + from_core * SIDE + line
                second = peer // SIDE * (2 * PEERS) + line * (2 * SIDE) + from_core * SIDE + peer % SIDE
                device = jnp.where(core == 0, first, second)
                out_ref[pl.ds(device, 1), :] = best_ref[row : row + 1, peer * CAP : (peer + 1) * CAP]


def finish(pos_ref, got_ref, out_ref):
    rng, rank = pos_ref[0:1, :], pos_ref[1:2, :]
    docs = rng.shape[1]
    first = got_ref[pl.ds(0, PEERS, stride=2 * SIDE), :]
    for line in range(1, SIDE):
        first = jnp.maximum(first, got_ref[pl.ds(line, PEERS, stride=2 * SIDE), :])
    second = []
    for z in range(SIDE):
        rows = [got_ref[pl.ds(z * 2 * PEERS + line * 2 * SIDE + SIDE, SIDE), :] for line in range(SIDE)]
        second.append(functools.reduce(jnp.maximum, rows))
    best = jnp.concatenate([first] + second, axis=0)
    pick = jnp.where(iota((best.shape[0], docs), 0) == rng, 1.0, 0.0)
    found = lax.dot_general(
        best, pick, (((0,), (0,)), ((), ())), precision=lax.Precision.HIGHEST, preferred_element_type=F32
    )
    out_ref[...] = jnp.sum(jnp.where(iota((CAP, docs), 0) == rank, found, 0.0), axis=0, keepdims=True)


def after(x, *others):
    return lax.optimization_barrier((x, *others))[0]


def per_device(embeddings, cluster_id):
    docs, columns = embeddings.shape
    devices = lax.axis_size("docs") * lax.axis_size("split")
    slots = jax.ShapeDtypeStruct((PEERS, CAP * columns // LANES + CODE_ROWS, LANES), BF16)

    pos, first, unit = pl.pallas_call(
        prepare,
        in_specs=[HBM, HBM],
        out_specs=[VMEM, HBM, HBM],
        out_shape=[
            jax.ShapeDtypeStruct((4, docs), jnp.int32),
            slots,
            jax.ShapeDtypeStruct((docs, columns), BF16),
        ],
        scratch_shapes=[
            pltpu.VMEM((docs, columns), F32),
            pltpu.VMEM((docs, columns), BF16),
            pltpu.VMEM(slots.shape, BF16),
            pltpu.SemaphoreType.DMA((8,)),
            pltpu.VMEM((1, docs), jnp.int32),
        ],
        compiler_params=PARAMS,
        name="prepare",
    )(pltpu.with_memory_space_constraint(cluster_id.reshape(1, docs), pltpu.HBM), pltpu.with_memory_space_constraint(embeddings, pltpu.HBM))

    other = pl.pallas_call(
        place_other,
        in_specs=[VMEM, VMEM],
        out_specs=VMEM,
        out_shape=slots,
        compiler_params=PARAMS,
        name="place_other",
    )(lax.ppermute(pos, AXES, core_moves()), lax.ppermute(unit, AXES, core_moves()))

    groups = plane_groups()
    moves_near = line_moves([(a, a - 1) for a in range(SIDE)])
    moves_far = line_moves([(a, a + 1) for a in range(SIDE)])

    def to_owner(x):
        return lax.all_to_all(x, AXES, 0, 0, axis_index_groups=groups, tiled=True)

    held = {}

    def score_call(state, new, pairs, name, loaded=(), last=False):
        names = sorted({holder(held, n) for some in pairs for p in some for n in p[:2]})
        table = jax.ShapeDtypeStruct((ROWS, PEERS * CAP), F32)
        extra = [jax.ShapeDtypeStruct(held[n].shape, BF16) for n in loaded[-1:]]
        scratch = [pltpu.VMEM(held[n].shape, BF16) for n in loaded[:-1]]
        if loaded:
            scratch.append(pltpu.SemaphoreType.DMA((len(loaded),)))
        out = pl.pallas_call(
            lambda *refs: scores(names, new, loaded, pairs, state[0] is pos, last, *refs),
            in_specs=[VMEM, VMEM] + [HBM if n in loaded else VMEM for n in names],
            out_specs=[VMEM] * (1 if last else 2 + len(extra)),
            out_shape=[jax.ShapeDtypeStruct((devices, CAP), F32)] if last else [table, table, *extra],
            scratch_shapes=[pltpu.VMEM(table.shape, F32)] * 2 if last else scratch,
            compiler_params=SCORE_PARAMS,
            name=name,
        )(*state[:2], *[held[n] for n in names])
        held.update(zip(loaded[-1:], out[2:]))
        return out

    def blocks(role, kind, start=0, end=PEERS):
        return [(role, kind, p, min(HALF, end - p)) for p in range(start, end, HALF)]

    def every(lefts, rights, when=ALWAYS):
        return [(a, b, when) for a in lefts for b in rights if a[:2] != b[:2] or a <= b]

    own_0, own_1, near_0, far_0 = blocks(OWN, 0), blocks(OWN, 1), blocks(NEAR, 0), blocks(FAR, 0)
    whole_0 = [(role, 0, 0, PEERS) for role in (OWN, NEAR, FAR)]
    own = to_owner(first)
    held[whole_0[0]] = own
    held[whole_0[1]] = lax.ppermute(own, AXES, moves_near)
    held[whole_0[2]] = lax.ppermute(own, AXES, moves_far)
    state = score_call((pos, pos), whole_0[:1], [every(own_0, own_0)], "scores_own_first")
    own = to_owner(other)
    whole_1 = (OWN, 1, 0, PEERS)
    held[whole_1] = own
    own = after(own, state[0])
    parts = ((0, 12), (12, 16))
    for number, (start, end) in enumerate(parts):
        held[NEAR, 1, start, end - start] = lax.ppermute(own[start:end], AXES, moves_near)
        half = (1 - number) * HALF
        held[FAR, 1, half, HALF] = lax.ppermute(own[half : half + HALF], AXES, moves_far)
        if not start:
            state = score_call(state, (whole_1,), [every(own_0, own_1) + every(own_1, own_1)], "scores_own")
            own = after(own, state[0])
    state = score_call(
        state,
        whole_0[1:],
        [
            every(own_0 + own_1, near_0),
            every(own_1, far_0) + every(near_0[:1], far_0, HEAVY) + every(near_0, far_0[1:], LIGHT),
        ],
        "scores_near_first",
        whole_0[1:],
    )
    older, (far_a, far_b) = [], blocks(FAR, 1)
    for number, (start, end) in enumerate(parts):
        near = blocks(NEAR, 1, start, end)
        older += near
        new = ((NEAR, 1, start, end - start),)
        pairs = every(own_1, near) + every(near, far_0)
        if not start:
            new += (far_b,)
            pairs += every([b for b in older if b[2] < HALF], [far_b], HEAVY) + every(older, [far_b], LIGHT)
        else:
            new += (far_a,)
            pairs += every([b for b in older if b[2] < HALF], [far_a], HEAVY) + every(near, [far_b], LIGHT)
        state = score_call(state, new, [pairs], f"scores_near_{start}", last=end == PEERS)
    got = lax.all_to_all(state[0], AXES, 0, 0, tiled=True)
    out = pl.pallas_call(
        finish,
        in_specs=[VMEM, VMEM],
        out_specs=VMEM,
        out_shape=jax.ShapeDtypeStruct((1, docs), F32),
        compiler_params=PARAMS,
        name="finish",
    )(pos, got)
    return out.reshape(docs)


def solution(mesh):
    return jax.shard_map(
        per_device,
        mesh=mesh,
        in_specs=(P(AXES, None), P(AXES)),
        out_specs=P(AXES),
        check_vma=False,
    )
```

```python
import functools

import jax
import jax.numpy as jnp
from jax import lax
from jax.experimental import pallas as pl
from jax.experimental.pallas import tpu as pltpu
from jax.sharding import PartitionSpec as P

F32 = jnp.float32
BF16 = jnp.bfloat16
CLU_DEV = 4
EPSILON = 1e-06
SIDE = 4
PEERS = SIDE * SIDE
CAP = 64
LANES = 128
CODE_ROWS = 8
HALF = PEERS // 2
ROWS = 8
CHUNKS = ((0, 0, 64), (1, 0, 48), (1, 48, 16))
BLOCKS = (((0, 32), (32, 32)), ((0, 32), (32, 16)), ((0, 16),))
OWN, NEAR, FAR = 0, 1, 2
LIGHT, HEAVY, ALWAYS = 0, 1, 2
AXES = ("docs", "split")
NT = (((1,), (1,)), ((), ()))
NN = (((1,), (0,)), ((), ()))
VMEM = pl.BlockSpec(memory_space=pltpu.VMEM)
HBM = pl.BlockSpec(memory_space=pltpu.HBM)
PARAMS = pltpu.CompilerParams(vmem_limit_bytes=24 * 2**20)
SCORE_PARAMS = pltpu.CompilerParams(vmem_limit_bytes=28 * 2**20)


def iota(shape, axis):
    return lax.broadcasted_iota(jnp.int32, shape, axis)


def flat(x, y, z, core):
    return ((z % SIDE * SIDE + y % SIDE) * 2 + core) * SIDE + x % SIDE


def plane_groups():
    side = range(SIDE)
    first = [[flat(x, y, z, 0) for z in side for y in side] for x in side]
    return first + [[flat(x, y, z, 1) for z in side for x in side] for y in side]


def line_moves(steps):
    side = range(SIDE)
    out = [(flat(a, u, z, 0), flat(b, u, z, 0)) for a, b in steps for u in side for z in side]
    return out + [(flat(u, a, z, 1), flat(u, b, z, 1)) for a, b in steps for u in side for z in side]


def core_moves():
    side = range(SIDE)
    return [(flat(x, y, z, c), flat(x, y, z, 1 - c)) for x in side for y in side for z in side for c in (0, 1)]


def own_core():
    return lax.axis_index("docs") & 1


def own_spot():
    return jnp.where(own_core() == 0, lax.axis_index("split"), (lax.axis_index("docs") >> 1) & (SIDE - 1))


def place(unit, kind_rng, rank, ids, kind, out, peers):
    docs, columns = unit.shape
    count = peers.stop - peers.start
    owner = kind_rng - (kind * PEERS + peers.start)
    inside = (owner >= 0) & (owner < count) & (rank < CAP)
    row = jnp.where(inside, owner * CAP + rank, -1)
    pick = jnp.where(iota((count * CAP, docs), 0) == row, 1.0, 0.0).astype(BF16)
    rows = lax.dot_general(pick, unit, NN, preferred_element_type=F32).astype(BF16)
    for tile in range(columns // LANES):
        part = rows[:, tile * LANES : (tile + 1) * LANES]
        out[peers, tile * CAP : (tile + 1) * CAP, :] = part.reshape(count, CAP, LANES)
    code_peer = iota((count * CODE_ROWS, docs), 0) // CODE_ROWS
    owned = jnp.where(owner == code_peer, 1.0, 0.0).astype(BF16)
    code = jnp.where(iota((LANES, docs), 0) == rank, (ids & (CLU_DEV - 1)) + 1, 0).astype(F32).astype(BF16)
    codes = lax.dot_general(owned, code, NT, preferred_element_type=F32).astype(BF16)
    out[peers, CAP * columns // LANES :, :] = codes.reshape(count, CODE_ROWS, LANES)


def prepare(ids_hbm, emb_ref, pos_ref, first_hbm, unit_hbm, emb, unit, first_ref, sems, ids_ref):
    docs, columns = emb.shape
    parts = 4
    size = docs // parts
    copies = [
        pltpu.make_async_copy(emb_ref.at[pl.ds(p * size, size)], emb.at[pl.ds(p * size, size)], sems.at[p])
        for p in range(parts)
    ]
    ids_copy = pltpu.make_async_copy(ids_hbm, ids_ref, sems.at[parts])
    ids_copy.start()
    for copy in copies:
        copy.start()
    ids_copy.wait()
    ids = ids_ref[...]
    rng = ids >> 2
    key = (ids * docs + iota(ids.shape, 1)).astype(F32)
    base = (rng * (CLU_DEV * docs)).astype(F32)
    key_col = jnp.transpose(jnp.broadcast_to(key, (LANES, docs)))
    ranks = []
    for lane in range(0, docs, LANES):
        before = (key_col < key[:, lane : lane + LANES]) & (key_col >= base[:, lane : lane + LANES])
        ranks.append(jnp.sum(jnp.where(before, 1.0, 0.0), axis=0, keepdims=True))
    rank = jnp.concatenate(ranks, axis=1).astype(jnp.int32)
    pos_ref[0:1, :] = rng
    pos_ref[1:2, :] = rank
    for p in range(parts):
        copies[p].wait()
        rows = emb[p * size : (p + 1) * size, :]
        scaling = lax.rsqrt(jnp.mean(rows * rows, axis=1, keepdims=True) + EPSILON) * columns ** (-0.5)
        unit[p * size : (p + 1) * size, :] = (rows * scaling).astype(BF16)
    unit_copy = pltpu.make_async_copy(unit, unit_hbm, sems.at[parts + 1])
    unit_copy.start()
    kind_rng = rng ^ (own_core() * PEERS)
    pos_ref[2:3, :] = kind_rng
    pos_ref[3:4, :] = ids
    out_copies = []
    for part in range(2):
        peers = slice(part * HALF, (part + 1) * HALF)
        place(unit[...], kind_rng, rank, ids, 0, first_ref, peers)
        out_copies.append(
            pltpu.make_async_copy(
                first_ref.at[pl.ds(part * HALF, HALF)], first_hbm.at[pl.ds(part * HALF, HALF)], sems.at[parts + 2 + part]
            )
        )
        out_copies[-1].start()
    unit_copy.wait()
    for copy in out_copies:
        copy.wait()


def place_other(pos_ref, unit_ref, out_ref):
    place(unit_ref[...], pos_ref[2:3, :], pos_ref[1:2, :], pos_ref[3:4, :], 1, out_ref, slice(0, PEERS))


def slot_codes(ref):
    codes = ref[:, ref.shape[1] - CODE_ROWS :, :].astype(F32)[:, 0, :].astype(BF16)
    lane = iota((1, ref.shape[0] * CAP), 1)
    spread = jnp.where(iota((CAP, lane.shape[1]), 0) == lane % CAP, 1.0, 0.0).astype(BF16)
    wide = lax.dot_general(codes[:, :CAP], spread, NN, preferred_element_type=F32)
    return jnp.sum(jnp.where(iota(wide.shape, 0) == lane // CAP, wide, 0.0), axis=0, keepdims=True)


def block_rows(ref, start, peers):
    tiles = (ref.shape[1] - CODE_ROWS) // CAP
    parts = [ref[start : start + peers, t * CAP : (t + 1) * CAP, :].reshape(peers * CAP, LANES) for t in range(tiles)]
    return jnp.concatenate(parts, axis=1)


def holder(names, block):
    return next(n for n in names if n[:2] == block[:2] and n[2] <= block[2] < n[2] + n[3])


def scores(names, new, loaded, pairs, fresh, last, best_in_ref, codes_in_ref, *refs):
    arrays = dict(zip(names, refs[: len(names)]))
    refs = list(refs[len(names) :])
    if last:
        refs = [*refs[1:3], refs[0]]
    best_ref, codes_ref = refs[:2]
    copies = {}
    for number, name in enumerate(loaded):
        target = refs[2] if name == loaded[-1] else refs[3 + number]
        copies[name] = pltpu.make_async_copy(arrays[name], target, refs[-1].at[number])
        copies[name].start()
        arrays[name] = target
    if fresh:
        best_ref[...] = jnp.full(best_ref.shape, -1.0, F32)
        codes_ref[...] = jnp.zeros(codes_ref.shape, F32)
    else:
        best_ref[...] = best_in_ref[...]
        codes_ref[...] = codes_in_ref[...]

    def at(block):
        role, kind, start, peers = block
        return slice(role * 2 + kind, role * 2 + kind + 1), slice(start * CAP, (start + peers) * CAP)

    def rows_of(block):
        name = holder(names, block)
        return block_rows(arrays[name], block[2] - name[2], block[3])

    def arrive(name):
        if name in copies:
            copies.pop(name).wait()
        codes_ref[at(name)] = slot_codes(arrays[name])

    def into(block, values):
        best_ref[at(block)] = jnp.maximum(best_ref[at(block)], values)

    def run(some):
        for left in dict.fromkeys(p[0] for p in some):
            left_rows = rows_of(left)
            left_codes = codes_ref[at(left)]
            left_codes = jnp.where(left_codes > 0, left_codes, -1.0)
            left_codes = jnp.transpose(jnp.broadcast_to(left_codes, (LANES, left_codes.shape[1])))[:, :1]
            total = None
            for right in [p[1] for p in some if p[0] == left]:
                score = lax.dot_general(left_rows, rows_of(right), NT, preferred_element_type=F32)
                allowed = left_codes == codes_ref[at(right)]
                if left == right:
                    allowed = allowed & (iota(score.shape, 0) != iota(score.shape, 1))
                score = jnp.where(allowed, score, -1.0)
                into(right, jnp.max(score, axis=0, keepdims=True))
                if left != right:
                    for lane in range(0, score.shape[1], LANES):
                        part = score[:, lane : lane + LANES]
                        total = part if total is None else jnp.maximum(total, part)
            if total is not None:
                into(left, jnp.max(jnp.transpose(total), axis=0, keepdims=True))

    waiting = list(new)
    for some in pairs:
        for name in [n for n in waiting if any(holder(names, block) == n for p in some for block in p[:2])]:
            waiting.remove(name)
            arrive(name)
        run([p[:2] for p in some if p[2] == ALWAYS])
        for when in (HEAVY, LIGHT):
            part = [p[:2] for p in some if p[2] == when]
            if part:
                pl.when(((own_spot() + 1) & 2) == 2 * (1 - when))(functools.partial(run, part))
    if last:
        pack(best_ref, refs[2])


def pack(best_ref, out_ref):
    core, spot = own_core(), own_spot()
    out_ref[...] = jnp.full(out_ref.shape, -1.0, F32)
    for kind in range(2):
        from_core = core if kind == 0 else 1 - core
        for role, shift in ((OWN, 0), (NEAR, 1), (FAR, 3)):
            line = (spot + shift) % SIDE
            row = role * 2 + kind
            for peer in range(PEERS):
                first = peer * (2 * SIDE) + from_core * SIDE + line
                second = peer // SIDE * (2 * PEERS) + line * (2 * SIDE) + from_core * SIDE + peer % SIDE
                device = jnp.where(core == 0, first, second)
                out_ref[pl.ds(device, 1), :] = best_ref[row : row + 1, peer * CAP : (peer + 1) * CAP]


def finish(pos_ref, got_ref, out_ref):
    rng, rank = pos_ref[0:1, :], pos_ref[1:2, :]
    docs = rng.shape[1]
    first = got_ref[pl.ds(0, PEERS, stride=2 * SIDE), :]
    for line in range(1, SIDE):
        first = jnp.maximum(first, got_ref[pl.ds(line, PEERS, stride=2 * SIDE), :])
    second = []
    for z in range(SIDE):
        rows = [got_ref[pl.ds(z * 2 * PEERS + line * 2 * SIDE + SIDE, SIDE), :] for line in range(SIDE)]
        second.append(functools.reduce(jnp.maximum, rows))
    best = jnp.concatenate([first] + second, axis=0)
    pick = jnp.where(iota((best.shape[0], docs), 0) == rng, 1.0, 0.0).astype(BF16)
    found, rest = 0.0, best
    for _ in range(3):
        part = rest.astype(BF16)
        rest = rest - part.astype(F32)
        found = found + lax.dot_general(part, pick, (((0,), (0,)), ((), ())), preferred_element_type=F32)
    out_ref[...] = jnp.sum(jnp.where(iota((CAP, docs), 0) == rank, found, 0.0), axis=0, keepdims=True)


def after(x, *others):
    return lax.optimization_barrier((x, *others))[0]


def per_device(embeddings, cluster_id):
    docs, columns = embeddings.shape
    devices = lax.axis_size("docs") * lax.axis_size("split")
    slots = jax.ShapeDtypeStruct((PEERS, CAP * columns // LANES + CODE_ROWS, LANES), BF16)

    pos, first, unit = pl.pallas_call(
        prepare,
        in_specs=[HBM, HBM],
        out_specs=[VMEM, HBM, HBM],
        out_shape=[
            jax.ShapeDtypeStruct((4, docs), jnp.int32),
            slots,
            jax.ShapeDtypeStruct((docs, columns), BF16),
        ],
        scratch_shapes=[
            pltpu.VMEM((docs, columns), F32),
            pltpu.VMEM((docs, columns), BF16),
            pltpu.VMEM(slots.shape, BF16),
            pltpu.SemaphoreType.DMA((8,)),
            pltpu.VMEM((1, docs), jnp.int32),
        ],
        compiler_params=PARAMS,
        name="prepare",
    )(pltpu.with_memory_space_constraint(cluster_id.reshape(1, docs), pltpu.HBM), pltpu.with_memory_space_constraint(embeddings, pltpu.HBM))

    other = pl.pallas_call(
        place_other,
        in_specs=[VMEM, VMEM],
        out_specs=VMEM,
        out_shape=slots,
        compiler_params=PARAMS,
        name="place_other",
    )(lax.ppermute(pos, AXES, core_moves()), lax.ppermute(unit, AXES, core_moves()))

    groups = plane_groups()
    moves_near = line_moves([(a, a - 1) for a in range(SIDE)])
    moves_far = line_moves([(a, a + 1) for a in range(SIDE)])

    def to_owner(x):
        return lax.all_to_all(x, AXES, 0, 0, axis_index_groups=groups, tiled=True)

    held = {}

    def score_call(state, new, pairs, name, loaded=(), last=False):
        names = sorted({holder(held, n) for some in pairs for p in some for n in p[:2]})
        table = jax.ShapeDtypeStruct((ROWS, PEERS * CAP), F32)
        extra = [jax.ShapeDtypeStruct(held[n].shape, BF16) for n in loaded[-1:]]
        scratch = [pltpu.VMEM(held[n].shape, BF16) for n in loaded[:-1]]
        if loaded:
            scratch.append(pltpu.SemaphoreType.DMA((len(loaded),)))
        out = pl.pallas_call(
            lambda *refs: scores(names, new, loaded, pairs, state[0] is pos, last, *refs),
            in_specs=[VMEM, VMEM] + [HBM if n in loaded else VMEM for n in names],
            out_specs=[VMEM] * (1 if last else 2 + len(extra)),
            out_shape=[jax.ShapeDtypeStruct((devices, CAP), F32)] if last else [table, table, *extra],
            scratch_shapes=[pltpu.VMEM(table.shape, F32)] * 2 if last else scratch,
            compiler_params=SCORE_PARAMS,
            name=name,
        )(*state[:2], *[held[n] for n in names])
        held.update(zip(loaded[-1:], out[2:]))
        return out

    def blocks(role, kind, start=0, end=PEERS):
        return [(role, kind, p, min(HALF, end - p)) for p in range(start, end, HALF)]

    def every(lefts, rights, when=ALWAYS):
        return [(a, b, when) for a in lefts for b in rights if a[:2] != b[:2] or a <= b]

    own_0, own_1, near_0, far_0 = blocks(OWN, 0), blocks(OWN, 1), blocks(NEAR, 0), blocks(FAR, 0)
    whole_0 = [(role, 0, 0, PEERS) for role in (OWN, NEAR, FAR)]
    own = to_owner(first)
    held[whole_0[0]] = own
    held[whole_0[1]] = lax.ppermute(own, AXES, moves_near)
    held[whole_0[2]] = lax.ppermute(own, AXES, moves_far)
    state = score_call((pos, pos), whole_0[:1], [every(own_0, own_0)], "scores_own_first")
    own = to_owner(other)
    whole_1 = (OWN, 1, 0, PEERS)
    held[whole_1] = own
    own = after(own, state[0])
    parts = ((0, 12), (12, 16))
    for number, (start, end) in enumerate(parts):
        held[NEAR, 1, start, end - start] = lax.ppermute(own[start:end], AXES, moves_near)
        half = (1 - number) * HALF
        held[FAR, 1, half, HALF] = lax.ppermute(own[half : half + HALF], AXES, moves_far)
        if not start:
            state = score_call(state, (whole_1,), [every(own_0, own_1) + every(own_1, own_1)], "scores_own")
    state = score_call(
        state,
        whole_0[1:],
        [
            every(own_0 + own_1, near_0),
            every(own_1, far_0) + every(near_0[:1], far_0, HEAVY) + every(near_0, far_0[1:], LIGHT),
        ],
        "scores_near_first",
        whole_0[1:],
    )
    older, (far_a, far_b) = [], blocks(FAR, 1)
    for number, (start, end) in enumerate(parts):
        near = blocks(NEAR, 1, start, end)
        older += near
        new = ((NEAR, 1, start, end - start),)
        pairs = every(own_1, near) + every(near, far_0)
        if not start:
            new += (far_b,)
            pairs += every([b for b in older if b[2] < HALF], [far_b], HEAVY) + every(older, [far_b], LIGHT)
        else:
            new += (far_a,)
            pairs += every([b for b in older if b[2] < HALF], [far_a], HEAVY) + every(near, [far_b], LIGHT)
        state = score_call(state, new, [pairs], f"scores_near_{start}", last=end == PEERS)
    got = lax.all_to_all(state[0], AXES, 0, 0, tiled=True)
    out = pl.pallas_call(
        finish,
        in_specs=[VMEM, VMEM],
        out_specs=VMEM,
        out_shape=jax.ShapeDtypeStruct((1, docs), F32),
        compiler_params=PARAMS,
        name="finish",
    )(pos, got)
    return out.reshape(docs)


def solution(mesh):
    return jax.shard_map(
        per_device,
        mesh=mesh,
        in_specs=(P(AXES, None), P(AXES)),
        out_specs=P(AXES),
        check_vma=False,
    )
```

```python
import functools

import jax
import jax.numpy as jnp
from jax import lax
from jax.experimental import pallas as pl
from jax.experimental.pallas import tpu as pltpu
from jax.sharding import PartitionSpec as P

F32 = jnp.float32
BF16 = jnp.bfloat16
CLU_DEV = 4
EPSILON = 1e-06
SIDE = 4
PEERS = SIDE * SIDE
CAP = 64
LANES = 128
CODE_ROWS = 8
HALF = PEERS // 2
ROWS = 8
CHUNKS = ((0, 0, 64), (1, 0, 48), (1, 48, 16))
BLOCKS = (((0, 32), (32, 32)), ((0, 32), (32, 16)), ((0, 16),))
OWN, NEAR, FAR = 0, 1, 2
LIGHT, HEAVY, ALWAYS = 0, 1, 2
AXES = ("docs", "split")
NT = (((1,), (1,)), ((), ()))
NN = (((1,), (0,)), ((), ()))
VMEM = pl.BlockSpec(memory_space=pltpu.VMEM)
HBM = pl.BlockSpec(memory_space=pltpu.HBM)
PARAMS = pltpu.CompilerParams(vmem_limit_bytes=24 * 2**20)
SCORE_PARAMS = pltpu.CompilerParams(vmem_limit_bytes=20 * 2**20)


def iota(shape, axis):
    return lax.broadcasted_iota(jnp.int32, shape, axis)


def flat(x, y, z, core):
    return ((z % SIDE * SIDE + y % SIDE) * 2 + core) * SIDE + x % SIDE


def plane_groups():
    side = range(SIDE)
    first = [[flat(x, y, z, 0) for z in side for y in side] for x in side]
    return first + [[flat(x, y, z, 1) for z in side for x in side] for y in side]


def line_moves(steps):
    side = range(SIDE)
    out = [(flat(a, u, z, 0), flat(b, u, z, 0)) for a, b in steps for u in side for z in side]
    return out + [(flat(u, a, z, 1), flat(u, b, z, 1)) for a, b in steps for u in side for z in side]


def core_moves():
    side = range(SIDE)
    return [(flat(x, y, z, c), flat(x, y, z, 1 - c)) for x in side for y in side for z in side for c in (0, 1)]


def own_core():
    return lax.axis_index("docs") & 1


def own_spot():
    return jnp.where(own_core() == 0, lax.axis_index("split"), (lax.axis_index("docs") >> 1) & (SIDE - 1))


def place(unit, kind_rng, rank, ids, kind, out, peers):
    docs, columns = unit.shape
    count = peers.stop - peers.start
    owner = kind_rng - (kind * PEERS + peers.start)
    inside = (owner >= 0) & (owner < count) & (rank < CAP)
    row = jnp.where(inside, owner * CAP + rank, -1)
    pick = jnp.where(iota((count * CAP, docs), 0) == row, 1.0, 0.0).astype(BF16)
    rows = lax.dot_general(pick, unit, NN, preferred_element_type=F32).astype(BF16)
    for tile in range(columns // LANES):
        part = rows[:, tile * LANES : (tile + 1) * LANES]
        out[peers, tile * CAP : (tile + 1) * CAP, :] = part.reshape(count, CAP, LANES)
    code_peer = iota((count * CODE_ROWS, docs), 0) // CODE_ROWS
    owned = jnp.where(owner == code_peer, 1.0, 0.0).astype(BF16)
    code = jnp.where(iota((LANES, docs), 0) == rank, (ids & (CLU_DEV - 1)) + 1, 0).astype(F32).astype(BF16)
    codes = lax.dot_general(owned, code, NT, preferred_element_type=F32).astype(BF16)
    out[peers, CAP * columns // LANES :, :] = codes.reshape(count, CODE_ROWS, LANES)


def prepare(ids_hbm, emb_ref, pos_ref, first_hbm, unit_hbm, emb, unit, first_ref, sems, ids_ref):
    docs, columns = emb.shape
    parts = 4
    size = docs // parts
    copies = [
        pltpu.make_async_copy(emb_ref.at[pl.ds(p * size, size)], emb.at[pl.ds(p * size, size)], sems.at[p])
        for p in range(parts)
    ]
    ids_copy = pltpu.make_async_copy(ids_hbm, ids_ref, sems.at[parts])
    ids_copy.start()
    for copy in copies:
        copy.start()
    ids_copy.wait()
    ids = ids_ref[...]
    rng = ids >> 2
    key = (ids * docs + iota(ids.shape, 1)).astype(F32)
    base = (rng * (CLU_DEV * docs)).astype(F32)
    key_col = jnp.transpose(jnp.broadcast_to(key, (LANES, docs)))
    ranks = []
    for lane in range(0, docs, LANES):
        before = (key_col < key[:, lane : lane + LANES]) & (key_col >= base[:, lane : lane + LANES])
        ranks.append(jnp.sum(jnp.where(before, 1.0, 0.0), axis=0, keepdims=True))
    rank = jnp.concatenate(ranks, axis=1).astype(jnp.int32)
    pos_ref[0:1, :] = rng
    pos_ref[1:2, :] = rank
    for p in range(parts):
        copies[p].wait()
        rows = emb[p * size : (p + 1) * size, :]
        scaling = lax.rsqrt(jnp.mean(rows * rows, axis=1, keepdims=True) + EPSILON) * columns ** (-0.5)
        unit[p * size : (p + 1) * size, :] = (rows * scaling).astype(BF16)
    unit_copy = pltpu.make_async_copy(unit, unit_hbm, sems.at[parts + 1])
    unit_copy.start()
    kind_rng = rng ^ (own_core() * PEERS)
    pos_ref[2:3, :] = kind_rng
    pos_ref[3:4, :] = ids
    out_copies = []
    for part in range(2):
        peers = slice(part * HALF, (part + 1) * HALF)
        place(unit[...], kind_rng, rank, ids, 0, first_ref, peers)
        out_copies.append(
            pltpu.make_async_copy(
                first_ref.at[pl.ds(part * HALF, HALF)], first_hbm.at[pl.ds(part * HALF, HALF)], sems.at[parts + 2 + part]
            )
        )
        out_copies[-1].start()
    unit_copy.wait()
    for copy in out_copies:
        copy.wait()


def place_other(pos_ref, unit_ref, out_ref):
    place(unit_ref[...], pos_ref[2:3, :], pos_ref[1:2, :], pos_ref[3:4, :], 1, out_ref, slice(0, PEERS))


def slot_codes(ref):
    codes = ref[:, ref.shape[1] - CODE_ROWS :, :].astype(F32)[:, 0, :].astype(BF16)
    lane = iota((1, ref.shape[0] * CAP), 1)
    spread = jnp.where(iota((CAP, lane.shape[1]), 0) == lane % CAP, 1.0, 0.0).astype(BF16)
    wide = lax.dot_general(codes[:, :CAP], spread, NN, preferred_element_type=F32)
    return jnp.sum(jnp.where(iota(wide.shape, 0) == lane // CAP, wide, 0.0), axis=0, keepdims=True)


def block_rows(ref, start, peers):
    tiles = (ref.shape[1] - CODE_ROWS) // CAP
    parts = [ref[start : start + peers, t * CAP : (t + 1) * CAP, :].reshape(peers * CAP, LANES) for t in range(tiles)]
    return jnp.concatenate(parts, axis=1)


def holder(names, block):
    return next(n for n in names if n[:2] == block[:2] and n[2] <= block[2] < n[2] + n[3])


def scores(names, new, loaded, pairs, fresh, last, best_in_ref, codes_in_ref, *refs):
    arrays = dict(zip(names, refs[: len(names)]))
    refs = list(refs[len(names) :])
    if last:
        refs = [*refs[1:3], refs[0]]
    best_ref, codes_ref = refs[:2]
    copies = {}
    for number, name in enumerate(loaded):
        target = refs[2] if name == loaded[-1] else refs[3 + number]
        copies[name] = pltpu.make_async_copy(arrays[name], target, refs[-1].at[number])
        copies[name].start()
        arrays[name] = target
    if fresh:
        best_ref[...] = jnp.full(best_ref.shape, -1.0, F32)
        codes_ref[...] = jnp.zeros(codes_ref.shape, F32)
    else:
        best_ref[...] = best_in_ref[...]
        codes_ref[...] = codes_in_ref[...]

    def at(block):
        role, kind, start, peers = block
        return slice(role * 2 + kind, role * 2 + kind + 1), slice(start * CAP, (start + peers) * CAP)

    def rows_of(block):
        name = holder(names, block)
        return block_rows(arrays[name], block[2] - name[2], block[3])

    def arrive(name):
        if name in copies:
            copies.pop(name).wait()
        codes_ref[at(name)] = slot_codes(arrays[name])

    def into(block, values):
        best_ref[at(block)] = jnp.maximum(best_ref[at(block)], values)

    def run(some):
        for left in dict.fromkeys(p[0] for p in some):
            left_rows = rows_of(left)
            left_codes = codes_ref[at(left)]
            left_codes = jnp.where(left_codes > 0, left_codes, -1.0)
            left_codes = jnp.transpose(jnp.broadcast_to(left_codes, (LANES, left_codes.shape[1])))[:, :1]
            total = None
            for right in [p[1] for p in some if p[0] == left]:
                score = lax.dot_general(left_rows, rows_of(right), NT, preferred_element_type=F32)
                allowed = left_codes == codes_ref[at(right)]
                if left == right:
                    allowed = allowed & (iota(score.shape, 0) != iota(score.shape, 1))
                score = jnp.where(allowed, score, -1.0)
                into(right, jnp.max(score, axis=0, keepdims=True))
                if left != right:
                    for lane in range(0, score.shape[1], LANES):
                        part = score[:, lane : lane + LANES]
                        total = part if total is None else jnp.maximum(total, part)
            if total is not None:
                into(left, jnp.max(jnp.transpose(total), axis=0, keepdims=True))

    waiting = list(new)
    for some in pairs:
        for name in [n for n in waiting if any(holder(names, block) == n for p in some for block in p[:2])]:
            waiting.remove(name)
            arrive(name)
        run([p[:2] for p in some if p[2] == ALWAYS])
        for when in (HEAVY, LIGHT):
            part = [p[:2] for p in some if p[2] == when]
            if part:
                pl.when(((own_spot() + 1) & 2) == 2 * (1 - when))(functools.partial(run, part))
    if last:
        pack(best_ref, refs[2])


def pack(best_ref, out_ref):
    core, spot = own_core(), own_spot()
    out_ref[...] = jnp.full(out_ref.shape, -1.0, F32)
    for kind in range(2):
        from_core = core if kind == 0 else 1 - core
        for role, shift in ((OWN, 0), (NEAR, 1), (FAR, 3)):
            line = (spot + shift) % SIDE
            row = role * 2 + kind
            for peer in range(PEERS):
                first = peer * (2 * SIDE) + from_core * SIDE + line
                second = peer // SIDE * (2 * PEERS) + line * (2 * SIDE) + from_core * SIDE + peer % SIDE
                device = jnp.where(core == 0, first, second)
                out_ref[pl.ds(device, 1), :] = best_ref[row : row + 1, peer * CAP : (peer + 1) * CAP]


def finish(pos_ref, got_ref, out_ref):
    rng, rank = pos_ref[0:1, :], pos_ref[1:2, :]
    docs = rng.shape[1]
    first = got_ref[pl.ds(0, PEERS, stride=2 * SIDE), :]
    for line in range(1, SIDE):
        first = jnp.maximum(first, got_ref[pl.ds(line, PEERS, stride=2 * SIDE), :])
    second = []
    for z in range(SIDE):
        rows = [got_ref[pl.ds(z * 2 * PEERS + line * 2 * SIDE + SIDE, SIDE), :] for line in range(SIDE)]
        second.append(functools.reduce(jnp.maximum, rows))
    best = jnp.concatenate([first] + second, axis=0)
    pick = jnp.where(iota((best.shape[0], docs), 0) == rng, 1.0, 0.0).astype(BF16)
    found, rest = 0.0, best
    for _ in range(3):
        part = rest.astype(BF16)
        rest = rest - part.astype(F32)
        found = found + lax.dot_general(part, pick, (((0,), (0,)), ((), ())), preferred_element_type=F32)
    out_ref[...] = jnp.sum(jnp.where(iota((CAP, docs), 0) == rank, found, 0.0), axis=0, keepdims=True)


def after(x, *others):
    return lax.optimization_barrier((x, *others))[0]


def per_device(embeddings, cluster_id):
    docs, columns = embeddings.shape
    devices = lax.axis_size("docs") * lax.axis_size("split")
    slots = jax.ShapeDtypeStruct((PEERS, CAP * columns // LANES + CODE_ROWS, LANES), BF16)

    pos, first, unit = pl.pallas_call(
        prepare,
        in_specs=[HBM, HBM],
        out_specs=[VMEM, HBM, HBM],
        out_shape=[
            jax.ShapeDtypeStruct((4, docs), jnp.int32),
            slots,
            jax.ShapeDtypeStruct((docs, columns), BF16),
        ],
        scratch_shapes=[
            pltpu.VMEM((docs, columns), F32),
            pltpu.VMEM((docs, columns), BF16),
            pltpu.VMEM(slots.shape, BF16),
            pltpu.SemaphoreType.DMA((8,)),
            pltpu.VMEM((1, docs), jnp.int32),
        ],
        compiler_params=PARAMS,
        name="prepare",
    )(pltpu.with_memory_space_constraint(cluster_id.reshape(1, docs), pltpu.HBM), pltpu.with_memory_space_constraint(embeddings, pltpu.HBM))

    other = pl.pallas_call(
        place_other,
        in_specs=[VMEM, VMEM],
        out_specs=VMEM,
        out_shape=slots,
        compiler_params=PARAMS,
        name="place_other",
    )(lax.ppermute(pos, AXES, core_moves()), lax.ppermute(unit, AXES, core_moves()))

    groups = plane_groups()
    moves_near = line_moves([(a, a - 1) for a in range(SIDE)])
    moves_far = line_moves([(a, a + 1) for a in range(SIDE)])

    def to_owner(x):
        return lax.all_to_all(x, AXES, 0, 0, axis_index_groups=groups, tiled=True)

    held = {}

    def score_call(state, new, pairs, name, loaded=(), last=False):
        names = sorted({holder(held, n) for some in pairs for p in some for n in p[:2]})
        table = jax.ShapeDtypeStruct((ROWS, PEERS * CAP), F32)
        extra = [jax.ShapeDtypeStruct(held[n].shape, BF16) for n in loaded[-1:]]
        scratch = [pltpu.VMEM(held[n].shape, BF16) for n in loaded[:-1]]
        if loaded:
            scratch.append(pltpu.SemaphoreType.DMA((len(loaded),)))
        out = pl.pallas_call(
            lambda *refs: scores(names, new, loaded, pairs, state[0] is pos, last, *refs),
            in_specs=[VMEM, VMEM] + [HBM if n in loaded else VMEM for n in names],
            out_specs=[VMEM] * (1 if last else 2 + len(extra)),
            out_shape=[jax.ShapeDtypeStruct((devices, CAP), F32)] if last else [table, table, *extra],
            scratch_shapes=[pltpu.VMEM(table.shape, F32)] * 2 if last else scratch,
            compiler_params=SCORE_PARAMS,
            name=name,
        )(*state[:2], *[held[n] for n in names])
        held.update(zip(loaded[-1:], out[2:]))
        return out

    def blocks(role, kind, start=0, end=PEERS):
        return [(role, kind, p, min(HALF, end - p)) for p in range(start, end, HALF)]

    def every(lefts, rights, when=ALWAYS):
        return [(a, b, when) for a in lefts for b in rights if a[:2] != b[:2] or a <= b]

    own_0, own_1, near_0, far_0 = blocks(OWN, 0), blocks(OWN, 1), blocks(NEAR, 0), blocks(FAR, 0)
    whole_0 = [(role, 0, 0, PEERS) for role in (OWN, NEAR, FAR)]
    own = to_owner(first)
    held[whole_0[0]] = own
    held[whole_0[1]] = lax.ppermute(own, AXES, moves_near)
    held[whole_0[2]] = lax.ppermute(own, AXES, moves_far)
    state = score_call((pos, pos), whole_0[:1], [every(own_0, own_0)], "scores_own_first")
    own = to_owner(other)
    whole_1 = (OWN, 1, 0, PEERS)
    held[whole_1] = own
    own = after(own, state[0])
    parts = ((0, 12), (12, 16))
    for number, (start, end) in enumerate(parts):
        held[NEAR, 1, start, end - start] = lax.ppermute(own[start:end], AXES, moves_near)
        half = (1 - number) * HALF
        held[FAR, 1, half, HALF] = lax.ppermute(own[half : half + HALF], AXES, moves_far)
        if not start:
            state = score_call(state, (whole_1,), [every(own_0, own_1) + every(own_1, own_1)], "scores_own")
    state = score_call(
        state,
        whole_0[1:],
        [
            every(own_0 + own_1, near_0),
            every(own_1, far_0) + every(near_0[:1], far_0, HEAVY) + every(near_0, far_0[1:], LIGHT),
        ],
        "scores_near_first",
        whole_0[1:],
    )
    older, (far_a, far_b) = [], blocks(FAR, 1)
    for number, (start, end) in enumerate(parts):
        near = blocks(NEAR, 1, start, end)
        older += near
        new = ((NEAR, 1, start, end - start),)
        pairs = every(own_1, near) + every(near, far_0)
        if not start:
            new += (far_b,)
            pairs += every([b for b in older if b[2] < HALF], [far_b], HEAVY) + every(older, [far_b], LIGHT)
        else:
            new += (far_a,)
            pairs += every([b for b in older if b[2] < HALF], [far_a], HEAVY) + every(near, [far_b], LIGHT)
        state = score_call(state, new, [pairs], f"scores_near_{start}", last=end == PEERS)
    got = lax.all_to_all(state[0], AXES, 0, 0, tiled=True)
    out = pl.pallas_call(
        finish,
        in_specs=[VMEM, VMEM],
        out_specs=VMEM,
        out_shape=jax.ShapeDtypeStruct((1, docs), F32),
        compiler_params=PARAMS,
        name="finish",
    )(pos, got)
    return out.reshape(docs)


def solution(mesh):
    return jax.shard_map(
        per_device,
        mesh=mesh,
        in_specs=(P(AXES, None), P(AXES)),
        out_specs=P(AXES),
        check_vma=False,
    )
```
